32 devices in a mesh: batch: 4 (over y, core), seq: 8 (over z, x).
Axes of the slice: x: 2, y: 2, z: 4, core: 2. Of those that a mesh axis runs over, the one named last changes fastest.
Arguments:
- values: bfloat16 [1024, 8192], P(None, ('batch', 'seq')), may hold values from -6 to 6
- gates: bfloat16 [1024, 8192], P(None, ('batch', 'seq')), may hold values from -6 to 6
- cotangent: bfloat16 [1024, 8192], P(None, ('batch', 'seq')), may hold values from -12 to 12
- taps_values: float32 [3, 1024], replicated, may hold values from -3 to 3
- taps_gates: float32 [3, 1024], replicated, may hold values from -3 to 3
- skip_gain: float32 [1024], replicated, may hold values from 0.5 to 1.5
- twiddle: float32 [8, 1024], P('batch'), may hold values from 0.5 to 1.5
- mixing: float32 [8, 8], replicated, may hold values from -2 to 3
- spectrum: bfloat16 [1024, 8, 1024], P('seq', None, 'batch'), may hold values from -4 to 4
Outputs:
- mixed: bfloat16 [1024, 8192], P(None, ('batch', 'seq'))
- grad_values: bfloat16 [1024, 8192], P(None, ('batch', 'seq'))
- grad_gates: bfloat16 [1024, 8192], P(None, ('batch', 'seq'))
- grad_spectrum: float32 [1024, 8, 1024], P('seq', None, 'batch')
- grad_taps_values: float32 [3, 1024], P(None, 'seq')
- grad_taps_gates: float32 [3, 1024], P(None, 'seq')
- grad_skip: float32 [1024], P('seq')
The draws below stay inside these ranges and needn't reach their ends.
All inputs are finite; a program needn't handle non-finite values.
Results may differ from the reference program's by a relative error of at most 0.0085.
Values may be sent and summed in bfloat16 or wider, within the bound.
A program may use at most 64 MiB of HBM per device.

```python
import math
import jax
import jax.numpy as jnp
from jax import lax

D = 1024
BLOCK = 1024
LENGTH = 8192
BLOCKS = 8


def draw_cotangent(key, part):
    first_key = jax.random.fold_in(key, 0)
    base = jax.random.truncated_normal(first_key, -6.0, 6.0, (D, LENGTH), jnp.float32)
    along = 1.0 + 2.0 * jnp.arange(LENGTH, dtype=jnp.float32) / max(LENGTH - 1, 1)
    result = 0.5 * base * along[None, :]
    return result.astype(jnp.bfloat16)


def draw_mixing(key, part):
    positions = jnp.arange(BLOCKS, dtype=jnp.int32)
    diagonal = (positions[:, None] == positions[None, :]).astype(jnp.float32)
    noise = jax.random.truncated_normal(key, -3.0, 3.0, (BLOCKS, BLOCKS), jnp.float32)
    return diagonal + 0.6 / BLOCKS ** 0.5 * noise


def block_scale(own_key, shape, pieces, smallest, high):
    def one(axis_at, parts):
        steps = jax.random.uniform(jax.random.fold_in(jax.random.fold_in(own_key, 6), axis_at), (parts,), jnp.float32, smallest / len(pieces), high / len(pieces))
        return jnp.repeat(jnp.exp(steps), shape[axis_at] // parts).reshape((-1,) + (1,) * (len(shape) - axis_at - 1))

    factor_of = one(*pieces[0])
    for cut in pieces[1:]:
        factor_of = factor_of * one(*cut)
    return factor_of


def scatter_about(key, extent, scale, bound, shards=(), kind=jnp.bfloat16):
    values = jax.random.normal(key, extent, jnp.float32) * scale
    if len(shards) > 0:
        values = block_scale(key, extent, shards, -0.22, 0.18) * values
    return jnp.clip(values, min=-bound, max=bound).astype(kind)


def setup_inputs(seed: int = 0) -> dict:
    arg_keys = jax.random.split(jax.random.key(seed), 10)
    return {
        "values": scatter_about(arg_keys[0], (D, LENGTH), 1.0, 6.0, ((1, 32),)),
        "gates": scatter_about(arg_keys[1], (D, LENGTH), 1.0, 6.0, ((1, 32),)),
        "cotangent": draw_cotangent(jax.random.fold_in(arg_keys[9], 71), 0),
        "taps_values": scatter_about(arg_keys[3], (3, D), 0.6, 3.0, (), jnp.float32),
        "taps_gates": scatter_about(arg_keys[4], (3, D), 0.6, 3.0, (), jnp.float32),
        "skip_gain": jnp.clip(jax.random.uniform(arg_keys[5], (D,), jnp.float32, 0.5, 1.5), 0.5, 1.5),
        "twiddle": jnp.clip(0.5 + 1.0 * jax.random.uniform(arg_keys[6], (BLOCKS, BLOCK), jnp.float32) ** block_scale(arg_keys[6], (BLOCKS, BLOCK), ((0, 4),), -0.2, 0.2), 0.5, 1.5),
        "mixing": draw_mixing(jax.random.fold_in(arg_keys[9], 71), 0),
        "spectrum": scatter_about(arg_keys[8], (D, BLOCKS, BLOCK), 1.0, 4.0, ((0, 8), (2, 4))),
    }


def cas_table():
    indices = jnp.arange(BLOCK, dtype=jnp.int32)
    products = indices[:, None] * indices[None, :] % BLOCK
    angles = products.astype(jnp.float32) * (2.0 * math.pi / BLOCK)
    return ((jnp.cos(angles) + jnp.sin(angles)) / math.sqrt(BLOCK)).astype(jnp.bfloat16)

def transform(source, cas_matrix, twiddle, mixing):
    channels = source.shape[0]
    block_sums = jnp.dot(source.reshape(-1, BLOCK), cas_matrix, preferred_element_type=jnp.float32)
    block_sums = block_sums.reshape(channels, -1, BLOCK) * twiddle
    return jnp.einsum('pi,cik->cpk', mixing, block_sums, precision=lax.Precision.HIGHEST)

def back(spectra, cas_matrix, twiddle, mixing):
    channels = spectra.shape[0]
    weighted = jnp.einsum('ip,cik->cpk', mixing, spectra, precision=lax.Precision.HIGHEST) * twiddle
    weighted = weighted.astype(jnp.bfloat16)
    result = jnp.dot(weighted.reshape(-1, BLOCK), cas_matrix, preferred_element_type=jnp.float32)
    return result.reshape(channels, -1).astype(jnp.bfloat16)

def reference(values, gates, cotangent, taps_values, taps_gates, skip_gain, twiddle, mixing, spectrum):
    cas_matrix = cas_table()
    group_size = math.gcd(D, 64)
    group_count = D // group_size

    def split_rows(array):
        return array.reshape(group_count, group_size, LENGTH)

    def split_taps(taps):
        return taps.reshape(3, group_count, group_size).transpose(1, 0, 2)

    def one_group(inputs):
        value_rows, gate_rows, cot_rows, value_taps, gate_taps, skip_part, filter_part = inputs
        filters = filter_part.astype(jnp.float32)
        skip_col = skip_part[:, None]
        wide_values = jnp.pad(value_rows.astype(jnp.float32), ((0, 0), (2, 0)))
        wide_gates = jnp.pad(gate_rows.astype(jnp.float32), ((0, 0), (2, 0)))
        short_values = (value_taps[0][:, None] * wide_values[:, 2:] + value_taps[1][:, None] * wide_values[:, 1:-1] + value_taps[2][:, None] * wide_values[:, :-2]).astype(jnp.bfloat16)
        short_gates = gate_taps[0][:, None] * wide_gates[:, 2:] + gate_taps[1][:, None] * wide_gates[:, 1:-1] + gate_taps[2][:, None] * wide_gates[:, :-2]
        cotangent_f32 = cot_rows.astype(jnp.float32)
        grad_long = (cotangent_f32 * short_gates).astype(jnp.bfloat16)
        spectra_values = transform(short_values, cas_matrix, twiddle, mixing)
        long_values = back(spectra_values * filters, cas_matrix, twiddle, mixing)
        spectra_grads = transform(grad_long, cas_matrix, twiddle, mixing)
        back_grads = back(spectra_grads * filters, cas_matrix, twiddle, mixing)
        long_f32 = long_values.astype(jnp.float32)
        short_f32 = short_values.astype(jnp.float32)
        mixed = (short_gates * (long_f32 + skip_col * short_f32)).astype(jnp.bfloat16)
        grad_short_gates = cotangent_f32 * (long_f32 + skip_col * short_f32)
        long_grad_f32 = grad_long.astype(jnp.float32)
        grad_short_values = skip_col * long_grad_f32 + back_grads.astype(jnp.float32)
        ahead_values = jnp.pad(grad_short_values, ((0, 0), (0, 2)))
        ahead_gates = jnp.pad(grad_short_gates, ((0, 0), (0, 2)))
        grad_values = (value_taps[0][:, None] * ahead_values[:, :-2] + value_taps[1][:, None] * ahead_values[:, 1:-1] + value_taps[2][:, None] * ahead_values[:, 2:]).astype(jnp.bfloat16)
        grad_gates = (gate_taps[0][:, None] * ahead_gates[:, :-2] + gate_taps[1][:, None] * ahead_gates[:, 1:-1] + gate_taps[2][:, None] * ahead_gates[:, 2:]).astype(jnp.bfloat16)
        local_taps_values = jnp.stack([lax.optimization_barrier(jnp.sum(grad_short_values * wide_values[:, 2:], axis=1)), lax.optimization_barrier(jnp.sum(grad_short_values * wide_values[:, 1:-1], axis=1)), lax.optimization_barrier(jnp.sum(grad_short_values * wide_values[:, :-2], axis=1))], axis=0)
        local_taps_gates = jnp.stack([lax.optimization_barrier(jnp.sum(grad_short_gates * wide_gates[:, 2:], axis=1)), lax.optimization_barrier(jnp.sum(grad_short_gates * wide_gates[:, 1:-1], axis=1)), lax.optimization_barrier(jnp.sum(grad_short_gates * wide_gates[:, :-2], axis=1))], axis=0)
        local_skip = lax.optimization_barrier(jnp.sum(long_grad_f32 * short_f32, axis=1))
        grad_spectrum = spectra_values * spectra_grads
        return (mixed, grad_values, grad_gates, grad_spectrum, local_taps_values, local_taps_gates, local_skip)
    inputs = (split_rows(values), split_rows(gates), split_rows(cotangent), split_taps(taps_values), split_taps(taps_gates), skip_gain.reshape(group_count, group_size), spectrum.reshape(group_count, group_size, BLOCKS, BLOCK))
    results = lax.map(one_group, inputs)
    mixed = results[0].reshape(D, LENGTH)
    grad_values = results[1].reshape(D, LENGTH)
    grad_gates = results[2].reshape(D, LENGTH)
    grad_spectrum = results[3].reshape(D, BLOCKS, BLOCK)
    grad_taps_values = results[4].transpose(1, 0, 2).reshape(3, D)
    grad_taps_gates = results[5].transpose(1, 0, 2).reshape(3, D)
    grad_skip = results[6].reshape(D)
    return (mixed, grad_values, grad_gates, grad_spectrum, grad_taps_values, grad_taps_gates, grad_skip)
```

```python
import math

import jax
import jax.numpy as jnp
import numpy as np
from jax import lax
from jax.sharding import PartitionSpec as P

AXES = ("batch", "seq")


def cas_table(block):
    angles = np.arange(block, dtype=np.float32) * np.float32(2.0 * math.pi / block)
    entries = (np.cos(angles) + np.sin(angles)) / np.float32(math.sqrt(block))
    indices = np.arange(block)
    return jnp.asarray(entries.astype(jnp.bfloat16)[indices[:, None] * indices[None, :] % block])


def delayed(field, steps):
    return jnp.pad(field, ((0, 0), (steps, 0)))[:, : field.shape[1]]


def advanced(field, steps):
    return jnp.pad(field, ((0, 0), (0, steps)))[:, steps:]


def short_conv(field, taps, shift):
    return (
        taps[0][:, None] * field
        + taps[1][:, None] * shift(field, 1)
        + taps[2][:, None] * shift(field, 2)
    )


def tap_sums(gradient, field):
    return jnp.stack([jnp.sum(gradient * delayed(field, s), axis=1) for s in range(3)])


def per_device_plain(
    values, gates, cotangent, taps_values, taps_gates, skip_gain, twiddle, mixing, spectrum
):
    block = twiddle.shape[1]
    cas = cas_table(block)
    batch, seq = lax.axis_size("batch"), lax.axis_size("seq")
    share = values.shape[0] // (batch * seq)
    b, s = lax.axis_index("batch"), lax.axis_index("seq")
    start = (s * batch + b) * share
    stacked = jnp.stack([values, gates, cotangent])
    length_dev = values.shape[1]
    stacked = stacked.reshape(3, seq, batch, share, length_dev).transpose(2, 1, 0, 3, 4)
    stacked = stacked.reshape(batch * seq, 3, share, length_dev)
    whole = lax.all_to_all(stacked, AXES, split_axis=0, concat_axis=0, tiled=True)
    whole = whole.transpose(1, 2, 0, 3).reshape(3, share, -1)
    filters = lax.all_to_all(spectrum, "batch", split_axis=0, concat_axis=2, tiled=True)
    filters = filters.astype(jnp.float32)
    factors = lax.all_gather(twiddle, "batch", axis=0, tiled=True)
    params = jnp.concatenate([taps_values, taps_gates, skip_gain[None]], axis=0)
    params = lax.dynamic_slice_in_dim(params, start, share, 1)
    value_taps, gate_taps, skip = params[:3], params[3:6], params[6][:, None]
    field, gate, cot = (whole[n].astype(jnp.float32) for n in range(3))
    short_values = short_conv(field, value_taps, delayed).astype(jnp.bfloat16)
    short_gates = short_conv(gate, gate_taps, delayed)
    grad_long = (cot * short_gates).astype(jnp.bfloat16)

    def transform(source):
        sums = jnp.dot(source.reshape(-1, block), cas, preferred_element_type=jnp.float32)
        sums = sums.reshape(share, -1, block) * factors
        return jnp.einsum("pi,cik->cpk", mixing, sums, precision=lax.Precision.HIGHEST)

    def back(spectra):
        mixed = jnp.einsum("pi,cpk->cik", mixing, spectra, precision=lax.Precision.HIGHEST)
        weighted = (mixed * factors).astype(jnp.bfloat16)
        result = jnp.dot(weighted.reshape(-1, block), cas, preferred_element_type=jnp.float32)
        return result.reshape(share, -1).astype(jnp.bfloat16).astype(jnp.float32)

    spectra_values, spectra_grads = transform(short_values), transform(grad_long)
    long_values, back_grads = back(spectra_values * filters), back(spectra_grads * filters)
    grad_spectrum = (spectra_values * spectra_grads).astype(jnp.bfloat16)
    grad_spectrum = lax.all_to_all(grad_spectrum, "batch", split_axis=2, concat_axis=0, tiled=True)
    short_f32 = short_values.astype(jnp.float32)
    long_f32 = grad_long.astype(jnp.float32)
    inner = long_values + skip * short_f32
    grad_short_gates = cot * inner
    grad_short_values = skip * long_f32 + back_grads
    outs = jnp.stack([
        (short_gates * inner).astype(jnp.bfloat16),
        short_conv(grad_short_values, value_taps, advanced).astype(jnp.bfloat16),
        short_conv(grad_short_gates, gate_taps, advanced).astype(jnp.bfloat16),
    ])
    outs = outs.reshape(3, share, batch * seq, length_dev).transpose(2, 0, 1, 3)
    outs = lax.all_to_all(outs, AXES, split_axis=0, concat_axis=0, tiled=True)
    outs = outs.reshape(batch, seq, 3, share, length_dev).transpose(2, 1, 0, 3, 4)
    outs = outs.reshape(3, -1, length_dev)
    sums = jnp.concatenate([
        tap_sums(grad_short_values, field),
        tap_sums(grad_short_gates, gate),
        jnp.sum(long_f32 * short_f32, axis=1)[None],
    ])
    sums = lax.all_gather(sums, "batch", axis=1, tiled=True)
    return (
        outs[0], outs[1], outs[2], grad_spectrum.astype(jnp.float32), sums[:3], sums[3:6], sums[6]
    )


def solution(mesh):
    spread = P(None, AXES)
    in_specs = (
        spread, spread, spread, P(), P(), P(), P("batch", None), P(), P("seq", None, "batch")
    )
    out_specs = (
        spread, spread, spread, P("seq", None, "batch"), P(None, "seq"), P(None, "seq"), P("seq")
    )
    return jax.shard_map(
        per_device_plain, mesh=mesh, in_specs=in_specs, out_specs=out_specs, check_vma=False
    )
```

```python
import functools
import math

import jax
import jax.numpy as jnp
import numpy as np
from jax import lax
from jax.experimental import pallas as pl
from jax.experimental.pallas import tpu as pltpu
from jax.sharding import PartitionSpec as P

AXES = ("batch", "seq")


def cas_table(block):
    angles = np.arange(block, dtype=np.float32) * np.float32(2.0 * math.pi / block)
    entries = (np.cos(angles) + np.sin(angles)) / np.float32(math.sqrt(block))
    indices = np.arange(block)
    return jnp.asarray(entries.astype(jnp.bfloat16)[indices[:, None] * indices[None, :] % block])


def delayed(field, steps):
    return jnp.pad(field, ((0, 0), (steps, 0)))[:, : field.shape[1]]


def advanced(field, steps):
    return jnp.pad(field, ((0, 0), (0, steps)))[:, steps:]


def short_conv(field, taps, shift):
    return (
        taps[0][:, None] * field
        + taps[1][:, None] * shift(field, 1)
        + taps[2][:, None] * shift(field, 2)
    )


def tap_sums(gradient, field):
    return jnp.stack([jnp.sum(gradient * delayed(field, s), axis=1) for s in range(3)])


def per_device_plain(
    values, gates, cotangent, taps_values, taps_gates, skip_gain, twiddle, mixing, spectrum
):
    block = twiddle.shape[1]
    cas = cas_table(block)
    batch, seq = lax.axis_size("batch"), lax.axis_size("seq")
    share = values.shape[0] // (batch * seq)
    b, s = lax.axis_index("batch"), lax.axis_index("seq")
    start = (s * batch + b) * share
    stacked = jnp.stack([values, gates, cotangent])
    length_dev = values.shape[1]
    stacked = stacked.reshape(3, seq, batch, share, length_dev).transpose(2, 1, 0, 3, 4)
    stacked = stacked.reshape(batch * seq, 3, share, length_dev)
    whole = lax.all_to_all(stacked, AXES, split_axis=0, concat_axis=0, tiled=True)
    whole = whole.transpose(1, 2, 0, 3).reshape(3, share, -1)
    filters = lax.all_to_all(spectrum, "batch", split_axis=0, concat_axis=2, tiled=True)
    filters = filters.astype(jnp.float32)
    factors = lax.all_gather(twiddle, "batch", axis=0, tiled=True)
    params = jnp.concatenate([taps_values, taps_gates, skip_gain[None]], axis=0)
    params = lax.dynamic_slice_in_dim(params, start, share, 1)
    value_taps, gate_taps, skip = params[:3], params[3:6], params[6][:, None]
    field, gate, cot = (whole[n].astype(jnp.float32) for n in range(3))
    short_values = short_conv(field, value_taps, delayed).astype(jnp.bfloat16)
    short_gates = short_conv(gate, gate_taps, delayed)
    grad_long = (cot * short_gates).astype(jnp.bfloat16)

    def transform(source):
        sums = jnp.dot(source.reshape(-1, block), cas, preferred_element_type=jnp.float32)
        sums = sums.reshape(share, -1, block) * factors
        return jnp.einsum("pi,cik->cpk", mixing, sums, precision=lax.Precision.HIGHEST)

    def back(spectra):
        mixed = jnp.einsum("pi,cpk->cik", mixing, spectra, precision=lax.Precision.HIGHEST)
        weighted = (mixed * factors).astype(jnp.bfloat16)
        result = jnp.dot(weighted.reshape(-1, block), cas, preferred_element_type=jnp.float32)
        return result.reshape(share, -1).astype(jnp.bfloat16).astype(jnp.float32)

    spectra_values, spectra_grads = transform(short_values), transform(grad_long)
    long_values, back_grads = back(spectra_values * filters), back(spectra_grads * filters)
    grad_spectrum = (spectra_values * spectra_grads).astype(jnp.bfloat16)
    grad_spectrum = lax.all_to_all(grad_spectrum, "batch", split_axis=2, concat_axis=0, tiled=True)
    short_f32 = short_values.astype(jnp.float32)
    long_f32 = grad_long.astype(jnp.float32)
    inner = long_values + skip * short_f32
    grad_short_gates = cot * inner
    grad_short_values = skip * long_f32 + back_grads
    outs = jnp.stack([
        (short_gates * inner).astype(jnp.bfloat16),
        short_conv(grad_short_values, value_taps, advanced).astype(jnp.bfloat16),
        short_conv(grad_short_gates, gate_taps, advanced).astype(jnp.bfloat16),
    ])
    outs = outs.reshape(3, share, batch * seq, length_dev).transpose(2, 0, 1, 3)
    outs = lax.all_to_all(outs, AXES, split_axis=0, concat_axis=0, tiled=True)
    outs = outs.reshape(batch, seq, 3, share, length_dev).transpose(2, 1, 0, 3, 4)
    outs = outs.reshape(3, -1, length_dev)
    sums = jnp.concatenate([
        tap_sums(grad_short_values, field),
        tap_sums(grad_short_gates, gate),
        jnp.sum(long_f32 * short_f32, axis=1)[None],
    ])
    sums = lax.all_gather(sums, "batch", axis=1, tiled=True)
    return (
        outs[0], outs[1], outs[2], grad_spectrum.astype(jnp.float32), sums[:3], sums[3:6], sums[6]
    )


LANES = 128
MESH = pl.DeviceIdType.MESH


def whole_sequences(
    batch, seq,
    values, gates, cotangent, spectrum, twiddle, mixing, params, cas,
    mixed, grad_values, grad_gates, grad_spectrum, sums,
    fields, filters, factors, short_values, grad_long, wide, weighted, spectra, filtered, gradient,
    out_fields, out_spectrum, totals,
    in_send, in_recv, out_send, out_recv, side_send, side_recv,
):
    b, s = lax.axis_index("batch"), lax.axis_index("seq")
    count = batch * seq
    me = b * seq + s
    share, length = fields.shape[2], fields.shape[3]
    block = cas.shape[0]
    blocks = short_values.shape[0] // share
    per_block = block // length
    freqs = block // batch

    def rows_of(bt, st):
        return pl.ds(pl.multiple_of((st * batch + bt) * share, share), share)

    def batch_rows(bt):
        return pl.ds(pl.multiple_of(bt * share, share), share)

    def other(step):
        peer = lax.rem(me + step, count)
        return peer, lax.div(peer, seq), lax.rem(peer, seq)

    def each_other(body):
        @pl.loop(1, count)
        def _(step):
            body(*other(step))

    def each_batch(body):
        for step in range(1, batch):
            body(lax.rem(b + step, batch))

    barrier = pltpu.get_barrier_semaphore()
    each_other(lambda peer, bt, st: pl.semaphore_signal(
        barrier, inc=1, device_id=(bt, st), device_id_type=MESH))
    pl.semaphore_wait(barrier, count - 1)

    def in_copy(n, peer, bt, st, slot):
        return pltpu.make_async_remote_copy(
            src_ref=(values, gates, cotangent)[n].at[rows_of(bt, st), :],
            dst_ref=fields.at[n, me],
            send_sem=in_send.at[n, peer],
            recv_sem=in_recv.at[n, slot],
            device_id=(bt, st),
            device_id_type=MESH,
        )

    def out_copy(n, peer, bt, st, slot):
        return pltpu.make_async_remote_copy(
            src_ref=out_fields.at[n, peer],
            dst_ref=(mixed, grad_gates, grad_values)[n].at[rows_of(b, s), :],
            send_sem=out_send.at[n, peer],
            recv_sem=out_recv.at[n, slot],
            device_id=(bt, st),
            device_id_type=MESH,
        )

    def side_copy(n, bt, slot):
        source = (spectrum.at[:, batch_rows(bt), :], twiddle, out_spectrum.at[bt], sums.at[b])[n]
        target = (filters.at[b], factors.at[b], grad_spectrum.at[:, batch_rows(b), :], sums.at[b])[n]
        return pltpu.make_async_remote_copy(
            src_ref=source,
            dst_ref=target,
            send_sem=side_send.at[n, bt],
            recv_sem=side_recv.at[n, slot],
            device_id=(bt, s),
            device_id_type=MESH,
        )

    def start_in(n):
        each_other(lambda peer, bt, st: in_copy(n, peer, bt, st, me).start())

    def wait_in(n):
        each_other(lambda peer, bt, st: in_copy(n, peer, bt, st, peer).wait_recv())

    def start_out(n):
        each_other(lambda peer, bt, st: out_copy(n, peer, bt, st, me).start())
        (mixed, grad_gates, grad_values)[n][rows_of(b, s), :] = out_fields[n, me]

    start_in(0)
    each_batch(lambda bt: side_copy(1, bt, b).start())
    each_batch(lambda bt: side_copy(0, bt, b).start())
    start_in(1)
    start_in(2)
    for n, source in enumerate((values, gates, cotangent)):
        fields[n, me] = source[rows_of(b, s), :]
    filters[b] = spectrum[:, batch_rows(b), :]
    factors[b] = twiddle[...]
    totals[...] = jnp.zeros_like(totals)

    lane = lax.broadcasted_iota(jnp.int32, (share, length), 1)
    value_taps = [params[:, n : n + 1] for n in range(3)]
    gate_taps = [params[:, n : n + 1] for n in range(3, 6)]
    skip = params[:, 6:7]
    matrix = [[mixing[p, i] for i in range(blocks)] for p in range(blocks)]

    def delays(n, d):
        now = fields[n, d].astype(jnp.float32)
        before = fields[n, jnp.maximum(d - 1, 0)].astype(jnp.float32)
        before = jnp.where(d > 0, before, 0.0)
        return [now] + [
            jnp.where(lane < k, pltpu.roll(before, k, 1), pltpu.roll(now, k, 1)) for k in (1, 2)
        ]

    def advances(d):
        now = gradient[d]
        after = jnp.where(d < count - 1, gradient[jnp.minimum(d + 1, count - 1)], 0.0)
        return [now] + [
            jnp.where(
                lane >= length - k, pltpu.roll(after, length - k, 1), pltpu.roll(now, length - k, 1)
            )
            for k in (1, 2)
        ]

    def conv(taps, shifted):
        return taps[0] * shifted[0] + taps[1] * shifted[1] + taps[2] * shifted[2]

    def each_chunk(body):
        @pl.loop(0, blocks)
        def _(i):
            for q in range(per_block):
                rows = pl.ds(pl.multiple_of(i * share, share), share)
                body(i * per_block + q, rows, slice(q * length, (q + 1) * length))

    def times_table(source, target):
        tile = min(256, block)

        @pl.loop(0, block // tile)
        def _(at):
            columns = pl.ds(pl.multiple_of(at * tile, tile), tile)
            product = jnp.dot(source[...], cas[:, columns], preferred_element_type=jnp.float32)
            target[:, columns] = product.astype(target.dtype)

    def mix(of_values):
        group = 16

        @pl.loop(0, batch)
        def _(kt):
            for inside in range(0, freqs, LANES):
                columns = pl.ds(pl.multiple_of(kt * freqs + inside, LANES), LANES)
                part = slice(inside, inside + LANES)
                per_batch = blocks // batch
                factor = [
                    factors[i // per_batch, i % per_batch : i % per_batch + 1, columns]
                    for i in range(blocks)
                ]
                for first in range(0, share, group):
                    rows = slice(first, first + group)
                    sums_in = [
                        wide[i * share + first : i * share + first + group, columns] * factor[i]
                        for i in range(blocks)
                    ]
                    products = []
                    for p in range(blocks):
                        mine = matrix[p][0] * sums_in[0]
                        for i in range(1, blocks):
                            mine = mine + matrix[p][i] * sums_in[i]
                        at = slice(p * share + first, p * share + first + group)
                        if of_values:
                            spectra[at, columns] = mine
                        else:
                            out_spectrum[kt, p, rows, part] = (
                                spectra[at, columns] * mine
                            ).astype(out_spectrum.dtype)
                        products.append(mine * filters[kt, p, rows, part].astype(jnp.float32))
                    for i in range(blocks):
                        mine = matrix[0][i] * products[0]
                        for p in range(1, blocks):
                            mine = mine + matrix[p][i] * products[p]
                        weighted[i * share + first : i * share + first + group, columns] = (
                            mine * factor[i]
                        ).astype(weighted.dtype)

    wait_in(0)

    @each_chunk
    def _(d, rows, columns):
        short_values[rows, columns] = conv(value_taps, delays(0, d)).astype(short_values.dtype)

    times_table(short_values, wide)
    each_batch(lambda bt: side_copy(1, bt, bt).wait_recv())
    each_batch(lambda bt: side_copy(0, bt, bt).wait_recv())
    mix(True)
    times_table(weighted, filtered)

    wait_in(1)
    wait_in(2)

    @each_chunk
    def _(d, rows, columns):
        shifted = delays(1, d)
        short_gates = conv(gate_taps, shifted)
        cot = fields[2, d].astype(jnp.float32)
        short = short_values[rows, columns].astype(jnp.float32)
        inner = filtered[rows, columns].astype(jnp.float32) + skip * short
        out_fields[0, d] = (short_gates * inner).astype(out_fields.dtype)
        long = (cot * short_gates).astype(grad_long.dtype)
        grad_long[rows, columns] = long
        grads = cot * inner
        gradient[d] = grads
        for k in range(3):
            totals[3 + k] += grads * shifted[k]
        totals[6] += long.astype(jnp.float32) * short

    start_out(0)

    @each_chunk
    def _(d, rows, columns):
        out_fields[1, d] = conv(gate_taps, advances(d)).astype(out_fields.dtype)

    start_out(1)

    times_table(grad_long, wide)
    mix(False)
    each_batch(lambda bt: side_copy(2, bt, b).start())
    grad_spectrum[:, batch_rows(b), :] = out_spectrum[b]
    times_table(weighted, filtered)

    @each_chunk
    def _(d, rows, columns):
        grads = skip * grad_long[rows, columns].astype(jnp.float32)
        grads = grads + filtered[rows, columns].astype(jnp.float32)
        gradient[d] = grads
        shifted = delays(0, d)
        for k in range(3):
            totals[k] += grads * shifted[k]

    @each_chunk
    def _(d, rows, columns):
        out_fields[2, d] = conv(value_taps, advances(d)).astype(out_fields.dtype)

    start_out(2)
    column = lax.broadcasted_iota(jnp.int32, (share, LANES), 1)
    line = jnp.zeros((share, LANES), jnp.float32)
    for k in range(7):
        line = jnp.where(column == k, jnp.sum(totals[k], axis=1, keepdims=True), line)
    sums[b] = line
    each_batch(lambda bt: side_copy(3, bt, b).start())

    for n in range(3):
        each_other(lambda peer, bt, st: in_copy(n, peer, bt, st, me).wait_send())
        each_other(lambda peer, bt, st: out_copy(n, peer, bt, st, peer).wait_recv())
        each_other(lambda peer, bt, st: out_copy(n, peer, bt, st, me).wait_send())
    for n in range(4):
        if n >= 2:
            each_batch(lambda bt: side_copy(n, bt, bt).wait_recv())
        each_batch(lambda bt: side_copy(n, bt, b).wait_send())


def per_device_kernel(
    values, gates, cotangent, taps_values, taps_gates, skip_gain, twiddle, mixing, spectrum
):
    batch, seq = lax.axis_size("batch"), lax.axis_size("seq")
    count = batch * seq
    channels, length = values.shape
    share = channels // count
    blocks, block = mixing.shape[0], twiddle.shape[1]
    freqs = block // batch
    b, s = lax.axis_index("batch"), lax.axis_index("seq")
    params = jnp.concatenate([taps_values, taps_gates, skip_gain[None], skip_gain[None]], axis=0)
    params = lax.dynamic_slice_in_dim(params, (s * batch + b) * share, share, 1).T
    vmem = pl.BlockSpec(memory_space=pltpu.VMEM)
    smem = pl.BlockSpec(memory_space=pltpu.SMEM)
    field = jax.ShapeDtypeStruct((channels, length), jnp.bfloat16)
    rows = blocks * share
    mixed, grad_values, grad_gates, grad_spectrum, sums = pl.pallas_call(
        functools.partial(whole_sequences, batch, seq),
        out_shape=[
            field, field, field,
            jax.ShapeDtypeStruct((blocks, channels // seq, freqs), jnp.bfloat16),
            jax.ShapeDtypeStruct((batch, share, LANES), jnp.float32),
        ],
        in_specs=[vmem, vmem, vmem, vmem, vmem, smem, vmem, vmem],
        out_specs=[vmem] * 5,
        scratch_shapes=[
            pltpu.VMEM((3, count, share, length), jnp.bfloat16),
            pltpu.VMEM((batch, blocks, share, freqs), jnp.bfloat16),
            pltpu.VMEM((batch, blocks // batch, block), jnp.float32),
            pltpu.VMEM((rows, block), jnp.bfloat16),
            pltpu.VMEM((rows, block), jnp.bfloat16),
            pltpu.VMEM((rows, block), jnp.float32),
            pltpu.VMEM((rows, block), jnp.bfloat16),
            pltpu.VMEM((rows, block), jnp.float32),
            pltpu.VMEM((rows, block), jnp.bfloat16),
            pltpu.VMEM((count, share, length), jnp.float32),
            pltpu.VMEM((3, count, share, length), jnp.bfloat16),
            pltpu.VMEM((batch, blocks, share, freqs), jnp.bfloat16),
            pltpu.VMEM((7, share, length), jnp.float32),
            pltpu.SemaphoreType.DMA((3, count)),
            pltpu.SemaphoreType.DMA((3, count)),
            pltpu.SemaphoreType.DMA((3, count)),
            pltpu.SemaphoreType.DMA((3, count)),
            pltpu.SemaphoreType.DMA((4, batch)),
            pltpu.SemaphoreType.DMA((4, batch)),
        ],
        compiler_params=pltpu.CompilerParams(
            collective_id=0, has_side_effects=True, vmem_limit_bytes=48 * 2**20
        ),
    )(
        values, gates, cotangent, spectrum.transpose(1, 0, 2), twiddle, mixing, params,
        cas_table(block),
    )
    sums = sums.reshape(channels // seq, LANES).T
    grad_spectrum = grad_spectrum.transpose(1, 0, 2).astype(jnp.float32)
    return (
        mixed, grad_values, grad_gates, grad_spectrum, sums[:3], sums[3:6], sums[6]
    )


def per_device(values, *rest):
    twiddle, mixing = rest[5], rest[6]
    batch = lax.axis_size("batch")
    count = batch * lax.axis_size("seq")
    channels, length = values.shape
    block = twiddle.shape[1]
    fits = (
        channels % (count * 16) == 0
        and length % LANES == 0
        and block % length == 0
        and block % (batch * LANES) == 0
        and mixing.shape[0] % batch == 0
    )
    return (per_device_kernel if fits else per_device_plain)(values, *rest)


def solution(mesh):
    spread = P(None, AXES)
    in_specs = (
        spread, spread, spread, P(), P(), P(), P("batch", None), P(), P("seq", None, "batch")
    )
    out_specs = (
        spread, spread, spread, P("seq", None, "batch"), P(None, "seq"), P(None, "seq"), P("seq")
    )
    return jax.shard_map(
        per_device, mesh=mesh, in_specs=in_specs, out_specs=out_specs, check_vma=False
    )
```

```python
import functools
import math

import jax
import jax.numpy as jnp
import numpy as np
from jax import lax
from jax.experimental import pallas as pl
from jax.experimental.pallas import tpu as pltpu
from jax.sharding import PartitionSpec as P

AXES = ("batch", "seq")


def cas_table(block):
    angles = np.arange(block, dtype=np.float32) * np.float32(2.0 * math.pi / block)
    entries = (np.cos(angles) + np.sin(angles)) / np.float32(math.sqrt(block))
    indices = np.arange(block)
    return jnp.asarray(entries.astype(jnp.bfloat16)[indices[:, None] * indices[None, :] % block])


def delayed(field, steps):
    return jnp.pad(field, ((0, 0), (steps, 0)))[:, : field.shape[1]]


def advanced(field, steps):
    return jnp.pad(field, ((0, 0), (0, steps)))[:, steps:]


def short_conv(field, taps, shift):
    return (
        taps[0][:, None] * field
        + taps[1][:, None] * shift(field, 1)
        + taps[2][:, None] * shift(field, 2)
    )


def tap_sums(gradient, field):
    return jnp.stack([jnp.sum(gradient * delayed(field, s), axis=1) for s in range(3)])


def per_device_plain(
    values, gates, cotangent, taps_values, taps_gates, skip_gain, twiddle, mixing, spectrum
):
    block = twiddle.shape[1]
    cas = cas_table(block)
    batch, seq = lax.axis_size("batch"), lax.axis_size("seq")
    share = values.shape[0] // (batch * seq)
    b, s = lax.axis_index("batch"), lax.axis_index("seq")
    start = (s * batch + b) * share
    stacked = jnp.stack([values, gates, cotangent])
    length_dev = values.shape[1]
    stacked = stacked.reshape(3, seq, batch, share, length_dev).transpose(2, 1, 0, 3, 4)
    stacked = stacked.reshape(batch * seq, 3, share, length_dev)
    whole = lax.all_to_all(stacked, AXES, split_axis=0, concat_axis=0, tiled=True)
    whole = whole.transpose(1, 2, 0, 3).reshape(3, share, -1)
    filters = lax.all_to_all(spectrum, "batch", split_axis=0, concat_axis=2, tiled=True)
    filters = filters.astype(jnp.float32)
    factors = lax.all_gather(twiddle, "batch", axis=0, tiled=True)
    params = jnp.concatenate([taps_values, taps_gates, skip_gain[None]], axis=0)
    params = lax.dynamic_slice_in_dim(params, start, share, 1)
    value_taps, gate_taps, skip = params[:3], params[3:6], params[6][:, None]
    field, gate, cot = (whole[n].astype(jnp.float32) for n in range(3))
    short_values = short_conv(field, value_taps, delayed).astype(jnp.bfloat16)
    short_gates = short_conv(gate, gate_taps, delayed)
    grad_long = (cot * short_gates).astype(jnp.bfloat16)

    def transform(source):
        sums = jnp.dot(source.reshape(-1, block), cas, preferred_element_type=jnp.float32)
        sums = sums.reshape(share, -1, block) * factors
        return jnp.einsum("pi,cik->cpk", mixing, sums, precision=lax.Precision.HIGHEST)

    def back(spectra):
        mixed = jnp.einsum("pi,cpk->cik", mixing, spectra, precision=lax.Precision.HIGHEST)
        weighted = (mixed * factors).astype(jnp.bfloat16)
        result = jnp.dot(weighted.reshape(-1, block), cas, preferred_element_type=jnp.float32)
        return result.reshape(share, -1).astype(jnp.bfloat16).astype(jnp.float32)

    spectra_values, spectra_grads = transform(short_values), transform(grad_long)
    long_values, back_grads = back(spectra_values * filters), back(spectra_grads * filters)
    grad_spectrum = (spectra_values * spectra_grads).astype(jnp.bfloat16)
    grad_spectrum = lax.all_to_all(grad_spectrum, "batch", split_axis=2, concat_axis=0, tiled=True)
    short_f32 = short_values.astype(jnp.float32)
    long_f32 = grad_long.astype(jnp.float32)
    inner = long_values + skip * short_f32
    grad_short_gates = cot * inner
    grad_short_values = skip * long_f32 + back_grads
    outs = jnp.stack([
        (short_gates * inner).astype(jnp.bfloat16),
        short_conv(grad_short_values, value_taps, advanced).astype(jnp.bfloat16),
        short_conv(grad_short_gates, gate_taps, advanced).astype(jnp.bfloat16),
    ])
    outs = outs.reshape(3, share, batch * seq, length_dev).transpose(2, 0, 1, 3)
    outs = lax.all_to_all(outs, AXES, split_axis=0, concat_axis=0, tiled=True)
    outs = outs.reshape(batch, seq, 3, share, length_dev).transpose(2, 1, 0, 3, 4)
    outs = outs.reshape(3, -1, length_dev)
    sums = jnp.concatenate([
        tap_sums(grad_short_values, field),
        tap_sums(grad_short_gates, gate),
        jnp.sum(long_f32 * short_f32, axis=1)[None],
    ])
    sums = lax.all_gather(sums, "batch", axis=1, tiled=True)
    return (
        outs[0], outs[1], outs[2], grad_spectrum.astype(jnp.float32), sums[:3], sums[3:6], sums[6]
    )


LANES = 128
MESH = pl.DeviceIdType.MESH


def whole_sequences(
    batch, seq,
    values, gates_in, cotangent_in, spectrum, twiddle, mixing, params, cas_in,
    mixed, grad_values, grad_gates, grad_spectrum, sums, gate_sums,
    gates, cotangent, cas, fields, filters, factors, short_values, grad_long, wide, weighted,
    spectra, filtered, gradient, out_fields, out_spectrum, totals,
    short_gates, long_here, inner_here, gates_gradient, before, after, rims, line, parts, batch_parts,
    in_send, in_recv, out_send, out_recv, side_send, side_recv, rim_send, rim_recv,
    part_send, part_recv, local,
):
    b, s = lax.axis_index("batch"), lax.axis_index("seq")
    count = batch * seq
    me = b * seq + s
    share, length = fields.shape[2], fields.shape[3]
    block = cas.shape[0]
    blocks = short_values.shape[0] // share
    per_block = block // length
    freqs = block // batch

    def rows_of(bt, st):
        return pl.ds(pl.multiple_of((st * batch + bt) * share, share), share)

    def batch_rows(bt):
        return pl.ds(pl.multiple_of(bt * share, share), share)

    def other(step):
        peer = lax.rem(me + step, count)
        return peer, lax.div(peer, seq), lax.rem(peer, seq)

    def each_other(body):
        @pl.loop(1, count)
        def _(step):
            body(*other(step))

    def each_batch(body):
        for step in range(1, batch):
            body(lax.rem(b + step, batch))

    barrier = pltpu.get_barrier_semaphore()
    each_other(lambda peer, bt, st: pl.semaphore_signal(
        barrier, inc=1, device_id=(bt, st), device_id_type=MESH))
    pl.semaphore_wait(barrier, count - 1)

    def in_copy(n, peer, bt, st, slot):
        return pltpu.make_async_remote_copy(
            src_ref=(values, long_here)[n].at[rows_of(bt, st), :],
            dst_ref=fields.at[n, me],
            send_sem=in_send.at[n, peer],
            recv_sem=in_recv.at[n, slot],
            device_id=(bt, st),
            device_id_type=MESH,
        )

    def out_copy(n, peer, bt, st, slot):
        return pltpu.make_async_remote_copy(
            src_ref=out_fields.at[n, peer],
            dst_ref=(inner_here, grad_values)[n].at[rows_of(b, s), :],
            send_sem=out_send.at[n, peer],
            recv_sem=out_recv.at[n, slot],
            device_id=(bt, st),
            device_id_type=MESH,
        )

    def side_copy(n, bt, slot):
        source = (
            spectrum.at[:, batch_rows(bt), :], twiddle, out_spectrum.at[bt], sums.at[b], batch_parts.at[b]
        )[n]
        target = (
            filters.at[b], factors.at[b], grad_spectrum.at[:, batch_rows(b), :], sums.at[b], batch_parts.at[b]
        )[n]
        return pltpu.make_async_remote_copy(
            src_ref=source,
            dst_ref=target,
            send_sem=side_send.at[n, bt],
            recv_sem=side_recv.at[n, slot],
            device_id=(bt, s),
            device_id_type=MESH,
        )

    def rim_copy(n):
        peer = lax.rem(me + (1, count - 1)[n], count)
        return pltpu.make_async_remote_copy(
            src_ref=rims.at[n],
            dst_ref=rims.at[2 + n],
            send_sem=rim_send.at[n],
            recv_sem=rim_recv.at[n],
            device_id=(lax.div(peer, seq), lax.rem(peer, seq)),
            device_id_type=MESH,
        )

    width = values.shape[0] // seq

    def part_copy(st, slot):
        return pltpu.make_async_remote_copy(
            src_ref=parts.at[0, st],
            dst_ref=parts.at[1, s],
            send_sem=part_send.at[st],
            recv_sem=part_recv.at[slot],
            device_id=(b, st),
            device_id_type=MESH,
        )

    def each_seq(body):
        for step in range(1, seq):
            body(lax.rem(s + step, seq))

    def start_in(n):
        each_other(lambda peer, bt, st: in_copy(n, peer, bt, st, me).start())

    def wait_in(n):
        each_other(lambda peer, bt, st: in_copy(n, peer, bt, st, peer).wait_recv())

    def start_out(n):
        each_other(lambda peer, bt, st: out_copy(n, peer, bt, st, me).start())
        (inner_here, grad_values)[n][rows_of(b, s), :] = out_fields[n, me]

    load_gates = pltpu.make_async_copy(gates_in, gates, local.at[0])
    load_cotangent = pltpu.make_async_copy(cotangent_in, cotangent, local.at[1])
    load_cas = pltpu.make_async_copy(cas_in, cas, local.at[2])
    load_values = pltpu.make_async_copy(values.at[rows_of(b, s), :], fields.at[0, me], local.at[3])
    load_filters = pltpu.make_async_copy(
        spectrum.at[:, batch_rows(b), :], filters.at[b], local.at[4]
    )
    load_gates.start()
    load_cotangent.start()
    start_in(0)
    each_batch(lambda bt: side_copy(1, bt, b).start())
    each_batch(lambda bt: side_copy(0, bt, b).start())
    load_values.start()
    load_cas.start()
    load_filters.start()
    factors[b] = twiddle[...]
    totals[...] = jnp.zeros_like(totals)

    lane = lax.broadcasted_iota(jnp.int32, (share, length), 1)
    mine_rows = rows_of(b, s)
    value_taps = [params[mine_rows, n : n + 1] for n in range(3)]
    skip = params[mine_rows, 6:7]
    matrix = [[mixing[p, i] for i in range(blocks)] for p in range(blocks)]

    def delayed_by(now, earlier):
        return [now] + [
            jnp.where(lane < k, pltpu.roll(earlier, k, 1), pltpu.roll(now, k, 1)) for k in (1, 2)
        ]

    def advanced_by(now, later):
        return [now] + [
            jnp.where(
                lane >= length - k, pltpu.roll(later, length - k, 1), pltpu.roll(now, length - k, 1)
            )
            for k in (1, 2)
        ]

    def delays(d):
        now = fields[0, d].astype(jnp.float32)
        earlier = fields[0, jnp.maximum(d - 1, 0)].astype(jnp.float32)
        return delayed_by(now, jnp.where(d > 0, earlier, 0.0))

    def advances(d):
        later = jnp.where(d < count - 1, gradient[jnp.minimum(d + 1, count - 1)], 0.0)
        return advanced_by(gradient[d], later)

    def gate_taps(rows):
        return [params[rows, n : n + 1] for n in range(3, 6)]

    def each_group(body):
        @pl.loop(0, count)
        def _(g):
            body(pl.ds(pl.multiple_of(g * share, share), share))

    def conv(taps, shifted):
        return taps[0] * shifted[0] + taps[1] * shifted[1] + taps[2] * shifted[2]

    def each_chunk(body):
        @pl.loop(0, blocks)
        def _(i):
            for q in range(per_block):
                rows = pl.ds(pl.multiple_of(i * share, share), share)
                body(i * per_block + q, rows, slice(q * length, (q + 1) * length))

    def times_table(source, target):
        tile = min(256, block)

        @pl.loop(0, block // tile)
        def _(at):
            columns = pl.ds(pl.multiple_of(at * tile, tile), tile)
            product = jnp.dot(source[...], cas[:, columns], preferred_element_type=jnp.float32)
            target[:, columns] = product.astype(target.dtype)

    def mix(of_values):
        group = 16

        @pl.loop(0, batch)
        def _(kt):
            for inside in range(0, freqs, LANES):
                columns = pl.ds(pl.multiple_of(kt * freqs + inside, LANES), LANES)
                part = slice(inside, inside + LANES)
                per_batch = blocks // batch
                factor = [
                    factors[i // per_batch, i % per_batch : i % per_batch + 1, columns]
                    for i in range(blocks)
                ]
                for first in range(0, share, group):
                    rows = slice(first, first + group)
                    sums_in = [
                        wide[i * share + first : i * share + first + group, columns] * factor[i]
                        for i in range(blocks)
                    ]
                    products = []
                    for p in range(blocks):
                        mine = matrix[p][0] * sums_in[0]
                        for i in range(1, blocks):
                            mine = mine + matrix[p][i] * sums_in[i]
                        at = slice(p * share + first, p * share + first + group)
                        if of_values:
                            spectra[at, columns] = mine
                        else:
                            out_spectrum[kt, p, rows, part] = (
                                spectra[at, columns] * mine
                            ).astype(out_spectrum.dtype)
                        products.append(mine * filters[kt, p, rows, part].astype(jnp.float32))
                    for i in range(blocks):
                        mine = matrix[0][i] * products[0]
                        for p in range(1, blocks):
                            mine = mine + matrix[p][i] * products[p]
                        weighted[i * share + first : i * share + first + group, columns] = (
                            mine * factor[i]
                        ).astype(weighted.dtype)

    load_gates.wait()
    last = gates[:, length - LANES :].astype(jnp.float32).T
    rims[0] = last[LANES - 8 :, :]
    rim_copy(0).start()
    load_cotangent.wait()
    rim_copy(0).wait_recv()
    came = jnp.where(me > 0, rims[2], 0.0)
    padded = jnp.concatenate([jnp.zeros((LANES - 8, came.shape[1]), jnp.float32), came], axis=0)
    before[...] = jnp.zeros_like(before)
    before[:, length - LANES :] = padded.T

    @each_group
    def _(rows):
        shifted = delayed_by(gates[rows, :].astype(jnp.float32), before[rows, :])
        short = conv(gate_taps(rows), shifted)
        short_gates[rows, :] = short
        long_here[rows, :] = (cotangent[rows, :].astype(jnp.float32) * short).astype(long_here.dtype)

    start_in(1)
    fields[1, me] = long_here[rows_of(b, s), :]

    load_values.wait()
    wait_in(0)

    @each_chunk
    def _(d, rows, columns):
        short_values[rows, columns] = conv(value_taps, delays(d)).astype(short_values.dtype)

    load_cas.wait()
    times_table(short_values, wide)
    load_filters.wait()
    each_batch(lambda bt: side_copy(1, bt, bt).wait_recv())
    each_batch(lambda bt: side_copy(0, bt, bt).wait_recv())
    mix(True)
    times_table(weighted, filtered)

    @each_chunk
    def _(d, rows, columns):
        short = short_values[rows, columns].astype(jnp.float32)
        inner = filtered[rows, columns].astype(jnp.float32) + skip * short
        out_fields[0, d] = inner.astype(out_fields.dtype)

    start_out(0)

    wait_in(1)

    @each_chunk
    def _(d, rows, columns):
        grad_long[rows, columns] = fields[1, d]

    times_table(grad_long, wide)
    mix(False)
    each_batch(lambda bt: side_copy(2, bt, b).start())
    grad_spectrum[:, batch_rows(b), :] = out_spectrum[b]
    times_table(weighted, filtered)

    @each_chunk
    def _(d, rows, columns):
        grads = skip * grad_long[rows, columns].astype(jnp.float32)
        gradient[d] = grads + filtered[rows, columns].astype(jnp.float32)

    @each_chunk
    def _(d, rows, columns):
        out_fields[1, d] = conv(value_taps, advances(d)).astype(out_fields.dtype)

    start_out(1)

    @each_chunk
    def _(d, rows, columns):
        shifted = delays(d)
        grads = gradient[d]
        for k in range(3):
            totals[k] += grads * shifted[k]
        totals[3] += grad_long[rows, columns].astype(jnp.float32) * short_values[
            rows, columns
        ].astype(jnp.float32)

    column = lax.broadcasted_iota(jnp.int32, (share, LANES), 1)

    def in_columns(columns):
        result = jnp.zeros((share, LANES), jnp.float32)
        for k, value in enumerate(columns):
            result = jnp.where(column == k, jnp.sum(value, axis=1, keepdims=True), result)
        return result

    sums[b] = in_columns([totals[k] for k in range(4)])
    each_batch(lambda bt: side_copy(3, bt, b).start())

    each_other(lambda peer, bt, st: out_copy(0, peer, bt, st, peer).wait_recv())

    @each_group
    def _(rows):
        inner = inner_here[rows, :].astype(jnp.float32)
        mixed[rows, :] = (short_gates[rows, :] * inner).astype(mixed.dtype)
        grads = cotangent[rows, :].astype(jnp.float32) * inner
        gates_gradient[rows, :] = grads
        shifted = delayed_by(gates[rows, :].astype(jnp.float32), before[rows, :])
        line[rows, :] = in_columns([grads * shifted[k] for k in range(3)])

    rims[1] = gates_gradient[:, :LANES].T[:8, :]
    rim_copy(1).start()
    turned = line[...].T[:8, :]
    for st in range(seq):
        parts[0, st] = turned[:, st * width : (st + 1) * width]
    each_seq(lambda st: part_copy(st, s).start())
    parts[1, s] = parts[0, s]
    rim_copy(1).wait_recv()
    came = jnp.where(me < count - 1, rims[3], 0.0)
    padded = jnp.concatenate([came, jnp.zeros((LANES - 8, came.shape[1]), jnp.float32)], axis=0)
    after[...] = jnp.zeros_like(after)
    after[:, :LANES] = padded.T

    @each_group
    def _(rows):
        shifted = advanced_by(gates_gradient[rows, :], after[rows, :])
        grad_gates[rows, :] = conv(gate_taps(rows), shifted).astype(grad_gates.dtype)

    each_seq(lambda st: part_copy(st, st).wait_recv())
    total = parts[1, 0]
    for st in range(1, seq):
        total = total + parts[1, st]
    batch_parts[b] = total
    each_batch(lambda bt: side_copy(4, bt, b).start())
    each_batch(lambda bt: side_copy(4, bt, bt).wait_recv())
    total = batch_parts[0]
    for bt in range(1, batch):
        total = total + batch_parts[bt]
    gate_sums[...] = total

    each_seq(lambda st: part_copy(st, s).wait_send())
    for n in range(2):
        rim_copy(n).wait_send()
        each_other(lambda peer, bt, st: in_copy(n, peer, bt, st, me).wait_send())
        each_other(lambda peer, bt, st: out_copy(n, peer, bt, st, me).wait_send())
    for n in range(5):
        if n in (2, 3):
            each_batch(lambda bt: side_copy(n, bt, bt).wait_recv())
        each_batch(lambda bt: side_copy(n, bt, b).wait_send())
    each_other(lambda peer, bt, st: out_copy(1, peer, bt, st, peer).wait_recv())


def per_device_kernel(
    values, gates, cotangent, taps_values, taps_gates, skip_gain, twiddle, mixing, spectrum
):
    batch, seq = lax.axis_size("batch"), lax.axis_size("seq")
    count = batch * seq
    channels, length = values.shape
    share = channels // count
    blocks, block = mixing.shape[0], twiddle.shape[1]
    freqs = block // batch
    params = jnp.concatenate([taps_values, taps_gates, skip_gain[None], skip_gain[None]], axis=0).T
    vmem = pl.BlockSpec(memory_space=pltpu.VMEM)
    hbm = pl.BlockSpec(memory_space=pl.ANY)
    smem = pl.BlockSpec(memory_space=pltpu.SMEM)
    field = jax.ShapeDtypeStruct((channels, length), jnp.bfloat16)
    rows = blocks * share
    mixed, grad_values, grad_gates, grad_spectrum, sums, gate_sums = pl.pallas_call(
        functools.partial(whole_sequences, batch, seq),
        out_shape=[
            field, field, field,
            jax.ShapeDtypeStruct((blocks, channels // seq, freqs), jnp.bfloat16),
            jax.ShapeDtypeStruct((batch, share, LANES), jnp.float32),
            jax.ShapeDtypeStruct((8, channels // seq), jnp.float32),
        ],
        in_specs=[hbm, hbm, hbm, hbm, vmem, smem, vmem, hbm],
        out_specs=[vmem] * 6,
        scratch_shapes=[
            pltpu.VMEM((channels, length), jnp.bfloat16),
            pltpu.VMEM((channels, length), jnp.bfloat16),
            pltpu.VMEM((block, block), jnp.bfloat16),
            pltpu.VMEM((2, count, share, length), jnp.bfloat16),
            pltpu.VMEM((batch, blocks, share, freqs), jnp.bfloat16),
            pltpu.VMEM((batch, blocks // batch, block), jnp.float32),
            pltpu.VMEM((rows, block), jnp.bfloat16),
            pltpu.VMEM((rows, block), jnp.bfloat16),
            pltpu.VMEM((rows, block), jnp.float32),
            pltpu.VMEM((rows, block), jnp.bfloat16),
            pltpu.VMEM((rows, block), jnp.float32),
            pltpu.VMEM((rows, block), jnp.bfloat16),
            pltpu.VMEM((count, share, length), jnp.float32),
            pltpu.VMEM((2, count, share, length), jnp.bfloat16),
            pltpu.VMEM((batch, blocks, share, freqs), jnp.bfloat16),
            pltpu.VMEM((4, share, length), jnp.float32),
            pltpu.VMEM((channels, length), jnp.float32),
            pltpu.VMEM((channels, length), jnp.bfloat16),
            pltpu.VMEM((channels, length), jnp.bfloat16),
            pltpu.VMEM((channels, length), jnp.float32),
            pltpu.VMEM((channels, length), jnp.float32),
            pltpu.VMEM((channels, length), jnp.float32),
            pltpu.VMEM((4, 8, channels), jnp.float32),
            pltpu.VMEM((channels, LANES), jnp.float32),
            pltpu.VMEM((2, seq, 8, channels // seq), jnp.float32),
            pltpu.VMEM((batch, 8, channels // seq), jnp.float32),
            pltpu.SemaphoreType.DMA((2, count)),
            pltpu.SemaphoreType.DMA((2, count)),
            pltpu.SemaphoreType.DMA((2, count)),
            pltpu.SemaphoreType.DMA((2, count)),
            pltpu.SemaphoreType.DMA((5, batch)),
            pltpu.SemaphoreType.DMA((5, batch)),
            pltpu.SemaphoreType.DMA((2,)),
            pltpu.SemaphoreType.DMA((2,)),
            pltpu.SemaphoreType.DMA((seq,)),
            pltpu.SemaphoreType.DMA((seq,)),
            pltpu.SemaphoreType.DMA((5,)),
        ],
        compiler_params=pltpu.CompilerParams(
            collective_id=0, has_side_effects=True, vmem_limit_bytes=56 * 2**20
        ),
    )(
        values, gates, cotangent, spectrum.transpose(1, 0, 2), twiddle, mixing, params,
        cas_table(block),
    )
    sums = sums.reshape(channels // seq, LANES).T
    grad_spectrum = grad_spectrum.transpose(1, 0, 2).astype(jnp.float32)
    return (
        mixed, grad_values, grad_gates, grad_spectrum, sums[:3], gate_sums[:3], sums[3]
    )


def per_device(values, *rest):
    twiddle, mixing = rest[5], rest[6]
    batch = lax.axis_size("batch")
    count = batch * lax.axis_size("seq")
    channels, length = values.shape
    block = twiddle.shape[1]
    fits = (
        channels % (count * 16) == 0
        and length % LANES == 0
        and channels % (lax.axis_size("seq") * LANES) == 0
        and block % length == 0
        and block % (batch * LANES) == 0
        and mixing.shape[0] % batch == 0
    )
    return (per_device_kernel if fits else per_device_plain)(values, *rest)


def solution(mesh):
    spread = P(None, AXES)
    in_specs = (
        spread, spread, spread, P(), P(), P(), P("batch", None), P(), P("seq", None, "batch")
    )
    out_specs = (
        spread, spread, spread, P("seq", None, "batch"), P(None, "seq"), P(None, "seq"), P("seq")
    )
    return jax.shard_map(
        per_device, mesh=mesh, in_specs=in_specs, out_specs=out_specs, check_vma=False
    )
```

```python
import functools
import math

import jax
import jax.numpy as jnp
import numpy as np
from jax import lax
from jax.experimental import pallas as pl
from jax.experimental.pallas import tpu as pltpu
from jax.sharding import PartitionSpec as P

AXES = ("batch", "seq")


def cas_table(block):
    angles = np.arange(block, dtype=np.float32) * np.float32(2.0 * math.pi / block)
    entries = (np.cos(angles) + np.sin(angles)) / np.float32(math.sqrt(block))
    indices = np.arange(block)
    return jnp.asarray(entries.astype(jnp.bfloat16)[indices[:, None] * indices[None, :] % block])


def delayed(field, steps):
    return jnp.pad(field, ((0, 0), (steps, 0)))[:, : field.shape[1]]


def advanced(field, steps):
    return jnp.pad(field, ((0, 0), (0, steps)))[:, steps:]


def short_conv(field, taps, shift):
    return (
        taps[0][:, None] * field
        + taps[1][:, None] * shift(field, 1)
        + taps[2][:, None] * shift(field, 2)
    )


def tap_sums(gradient, field):
    return jnp.stack([jnp.sum(gradient * delayed(field, s), axis=1) for s in range(3)])


def per_device_plain(
    values, gates, cotangent, taps_values, taps_gates, skip_gain, twiddle, mixing, spectrum
):
    block = twiddle.shape[1]
    cas = cas_table(block)
    batch, seq = lax.axis_size("batch"), lax.axis_size("seq")
    share = values.shape[0] // (batch * seq)
    b, s = lax.axis_index("batch"), lax.axis_index("seq")
    start = (s * batch + b) * share
    stacked = jnp.stack([values, gates, cotangent])
    length_dev = values.shape[1]
    stacked = stacked.reshape(3, seq, batch, share, length_dev).transpose(2, 1, 0, 3, 4)
    stacked = stacked.reshape(batch * seq, 3, share, length_dev)
    whole = lax.all_to_all(stacked, AXES, split_axis=0, concat_axis=0, tiled=True)
    whole = whole.transpose(1, 2, 0, 3).reshape(3, share, -1)
    filters = lax.all_to_all(spectrum, "batch", split_axis=0, concat_axis=2, tiled=True)
    filters = filters.astype(jnp.float32)
    factors = lax.all_gather(twiddle, "batch", axis=0, tiled=True)
    params = jnp.concatenate([taps_values, taps_gates, skip_gain[None]], axis=0)
    params = lax.dynamic_slice_in_dim(params, start, share, 1)
    value_taps, gate_taps, skip = params[:3], params[3:6], params[6][:, None]
    field, gate, cot = (whole[n].astype(jnp.float32) for n in range(3))
    short_values = short_conv(field, value_taps, delayed).astype(jnp.bfloat16)
    short_gates = short_conv(gate, gate_taps, delayed)
    grad_long = (cot * short_gates).astype(jnp.bfloat16)

    def transform(source):
        sums = jnp.dot(source.reshape(-1, block), cas, preferred_element_type=jnp.float32)
        sums = sums.reshape(share, -1, block) * factors
        return jnp.einsum("pi,cik->cpk", mixing, sums, precision=lax.Precision.HIGHEST)

    def back(spectra):
        mixed = jnp.einsum("pi,cpk->cik", mixing, spectra, precision=lax.Precision.HIGHEST)
        weighted = (mixed * factors).astype(jnp.bfloat16)
        result = jnp.dot(weighted.reshape(-1, block), cas, preferred_element_type=jnp.float32)
        return result.reshape(share, -1).astype(jnp.bfloat16).astype(jnp.float32)

    spectra_values, spectra_grads = transform(short_values), transform(grad_long)
    long_values, back_grads = back(spectra_values * filters), back(spectra_grads * filters)
    grad_spectrum = (spectra_values * spectra_grads).astype(jnp.bfloat16)
    grad_spectrum = lax.all_to_all(grad_spectrum, "batch", split_axis=2, concat_axis=0, tiled=True)
    short_f32 = short_values.astype(jnp.float32)
    long_f32 = grad_long.astype(jnp.float32)
    inner = long_values + skip * short_f32
    grad_short_gates = cot * inner
    grad_short_values = skip * long_f32 + back_grads
    outs = jnp.stack([
        (short_gates * inner).astype(jnp.bfloat16),
        short_conv(grad_short_values, value_taps, advanced).astype(jnp.bfloat16),
        short_conv(grad_short_gates, gate_taps, advanced).astype(jnp.bfloat16),
    ])
    outs = outs.reshape(3, share, batch * seq, length_dev).transpose(2, 0, 1, 3)
    outs = lax.all_to_all(outs, AXES, split_axis=0, concat_axis=0, tiled=True)
    outs = outs.reshape(batch, seq, 3, share, length_dev).transpose(2, 1, 0, 3, 4)
    outs = outs.reshape(3, -1, length_dev)
    sums = jnp.concatenate([
        tap_sums(grad_short_values, field),
        tap_sums(grad_short_gates, gate),
        jnp.sum(long_f32 * short_f32, axis=1)[None],
    ])
    sums = lax.all_gather(sums, "batch", axis=1, tiled=True)
    return (
        outs[0], outs[1], outs[2], grad_spectrum.astype(jnp.float32), sums[:3], sums[3:6], sums[6]
    )


LANES = 128
MESH = pl.DeviceIdType.MESH


def whole_sequences(
    batch, seq,
    values, gates_in, cotangent_in, spectrum, twiddle, mixing, value_taps_in, gate_taps_in, skip_in, cas_in,
    mixed, grad_values, grad_gates, grad_spectrum, value_sums, gate_sums, skip_sums,
    gates, cotangent, cas, params, turned_params, filters_landed, unpacked, spectrum_landed, sums,
    fields, filters, factors, short_values, grad_long, wide, weighted,
    spectra, filtered, gradient, out_fields, out_spectrum, totals,
    short_gates, long_here, inner_here, gates_gradient, before, after, rims, line, parts, batch_parts,
    in_send, in_recv, out_send, out_recv, side_send, side_recv, rim_send, rim_recv,
    part_send, part_recv, local,
):
    b, s = lax.axis_index("batch"), lax.axis_index("seq")
    count = batch * seq
    me = b * seq + s
    share, length = fields.shape[2], fields.shape[3]
    block = cas.shape[0]
    blocks = short_values.shape[0] // share
    per_block = block // length
    freqs = block // batch

    def rows_of(bt, st):
        return pl.ds(pl.multiple_of((st * batch + bt) * share, share), share)

    def batch_rows(bt):
        return pl.ds(pl.multiple_of(bt * share, share), share)

    def other(step):
        peer = lax.rem(me + step, count)
        return peer, lax.div(peer, seq), lax.rem(peer, seq)

    def each_other(body):
        @pl.loop(1, count)
        def _(step):
            body(*other(step))

    def each_batch(body):
        for step in range(1, batch):
            body(lax.rem(b + step, batch))

    load_gates = pltpu.make_async_copy(gates_in, gates, local.at[0])
    load_cotangent = pltpu.make_async_copy(cotangent_in, cotangent, local.at[1])
    load_cas = pltpu.make_async_copy(cas_in, cas, local.at[2])
    load_values = pltpu.make_async_copy(values.at[rows_of(b, s), :], fields.at[0, me], local.at[3])
    load_filters = pltpu.make_async_copy(
        spectrum.at[batch_rows(b)], filters_landed.at[b], local.at[4]
    )

    barrier = pltpu.get_barrier_semaphore()
    each_other(lambda peer, bt, st: pl.semaphore_signal(
        barrier, inc=1, device_id=(bt, st), device_id_type=MESH))
    load_gates.start()
    load_cotangent.start()
    load_values.start()
    load_cas.start()
    load_filters.start()
    turned_params[...] = jnp.zeros_like(turned_params)
    turned_params[0:3, :] = value_taps_in[...]
    turned_params[3:6, :] = gate_taps_in[...]
    turned_params[6:7, :] = skip_in[...]
    params[...] = turned_params[...].T
    load_gates.wait()
    rims[0] = gates[:, length - LANES :].astype(jnp.float32).T[LANES - 8 :, :]
    pl.semaphore_wait(barrier, count - 1)

    def in_copy(n, peer, bt, st, slot):
        return pltpu.make_async_remote_copy(
            src_ref=(values, long_here)[n].at[rows_of(bt, st), :],
            dst_ref=fields.at[n, me],
            send_sem=in_send.at[n, peer],
            recv_sem=in_recv.at[n, slot],
            device_id=(bt, st),
            device_id_type=MESH,
        )

    def out_copy(n, peer, bt, st, slot):
        return pltpu.make_async_remote_copy(
            src_ref=out_fields.at[n, peer],
            dst_ref=(inner_here, grad_values)[n].at[rows_of(b, s), :],
            send_sem=out_send.at[n, peer],
            recv_sem=out_recv.at[n, slot],
            device_id=(bt, st),
            device_id_type=MESH,
        )

    def side_copy(n, bt, slot):
        source = (
            spectrum.at[batch_rows(bt)], twiddle, out_spectrum.at[bt], sums.at[b], batch_parts.at[b]
        )[n]
        target = (
            filters_landed.at[b], factors.at[b], spectrum_landed.at[:, batch_rows(b), :], sums.at[b], batch_parts.at[b]
        )[n]
        return pltpu.make_async_remote_copy(
            src_ref=source,
            dst_ref=target,
            send_sem=side_send.at[n, bt],
            recv_sem=side_recv.at[n, slot],
            device_id=(bt, s),
            device_id_type=MESH,
        )

    def rim_copy(n):
        peer = lax.rem(me + (1, count - 1)[n], count)
        return pltpu.make_async_remote_copy(
            src_ref=rims.at[n],
            dst_ref=rims.at[2 + n],
            send_sem=rim_send.at[n],
            recv_sem=rim_recv.at[n],
            device_id=(lax.div(peer, seq), lax.rem(peer, seq)),
            device_id_type=MESH,
        )

    width = values.shape[0] // seq

    def part_copy(st, slot):
        return pltpu.make_async_remote_copy(
            src_ref=parts.at[0, st],
            dst_ref=parts.at[1, s],
            send_sem=part_send.at[st],
            recv_sem=part_recv.at[slot],
            device_id=(b, st),
            device_id_type=MESH,
        )

    def each_seq(body):
        for step in range(1, seq):
            body(lax.rem(s + step, seq))

    def start_in(n):
        each_other(lambda peer, bt, st: in_copy(n, peer, bt, st, me).start())

    def wait_in(n):
        each_other(lambda peer, bt, st: in_copy(n, peer, bt, st, peer).wait_recv())

    def start_out(n):
        each_other(lambda peer, bt, st: out_copy(n, peer, bt, st, me).start())
        (inner_here, grad_values)[n][rows_of(b, s), :] = out_fields[n, me]

    rim_copy(0).start()
    start_in(0)
    each_batch(lambda bt: side_copy(1, bt, b).start())
    each_batch(lambda bt: side_copy(0, bt, b).start())
    factors[b] = twiddle[...]
    totals[...] = jnp.zeros_like(totals)

    lane = lax.broadcasted_iota(jnp.int32, (share, length), 1)
    mine_rows = rows_of(b, s)
    value_taps = [params[mine_rows, n : n + 1] for n in range(3)]
    skip = params[mine_rows, 6:7]
    matrix = [[mixing[p, i] for i in range(blocks)] for p in range(blocks)]

    def delayed_by(now, earlier):
        return [now] + [
            jnp.where(lane < k, pltpu.roll(earlier, k, 1), pltpu.roll(now, k, 1)) for k in (1, 2)
        ]

    def advanced_by(now, later):
        return [now] + [
            jnp.where(
                lane >= length - k, pltpu.roll(later, length - k, 1), pltpu.roll(now, length - k, 1)
            )
            for k in (1, 2)
        ]

    def delays(d):
        now = fields[0, d].astype(jnp.float32)
        earlier = fields[0, jnp.maximum(d - 1, 0)].astype(jnp.float32)
        return delayed_by(now, jnp.where(d > 0, earlier, 0.0))

    def advances(d):
        later = jnp.where(d < count - 1, gradient[jnp.minimum(d + 1, count - 1)], 0.0)
        return advanced_by(gradient[d], later)

    def gate_taps(rows):
        return [params[rows, n : n + 1] for n in range(3, 6)]

    def each_group(body):
        @pl.loop(0, count)
        def _(g):
            body(pl.ds(pl.multiple_of(g * share, share), share))

    def conv(taps, shifted):
        return taps[0] * shifted[0] + taps[1] * shifted[1] + taps[2] * shifted[2]

    def each_chunk(body):
        @pl.loop(0, blocks)
        def _(i):
            for q in range(per_block):
                rows = pl.ds(pl.multiple_of(i * share, share), share)
                body(i * per_block + q, rows, slice(q * length, (q + 1) * length))

    def times_table(source, target):
        tile = min(256, block)

        @pl.loop(0, block // tile)
        def _(at):
            columns = pl.ds(pl.multiple_of(at * tile, tile), tile)
            product = jnp.dot(source[...], cas[:, columns], preferred_element_type=jnp.float32)
            target[:, columns] = product.astype(target.dtype)

    def mix(of_values):
        group = 16

        @pl.loop(0, batch)
        def _(kt):
            for inside in range(0, freqs, LANES):
                columns = pl.ds(pl.multiple_of(kt * freqs + inside, LANES), LANES)
                part = slice(inside, inside + LANES)
                per_batch = blocks // batch
                factor = [
                    factors[i // per_batch, i % per_batch : i % per_batch + 1, columns]
                    for i in range(blocks)
                ]
                for first in range(0, share, group):
                    rows = slice(first, first + group)
                    sums_in = [
                        wide[i * share + first : i * share + first + group, columns] * factor[i]
                        for i in range(blocks)
                    ]
                    products = []
                    for p in range(blocks):
                        mine = matrix[p][0] * sums_in[0]
                        for i in range(1, blocks):
                            mine = mine + matrix[p][i] * sums_in[i]
                        at = slice(p * share + first, p * share + first + group)
                        if of_values:
                            spectra[at, columns] = mine
                        else:
                            out_spectrum[kt, p, rows, part] = (
                                spectra[at, columns] * mine
                            ).astype(out_spectrum.dtype)
                        products.append(mine * filters[kt, p, rows, part])
                    for i in range(blocks):
                        mine = matrix[0][i] * products[0]
                        for p in range(1, blocks):
                            mine = mine + matrix[p][i] * products[p]
                        weighted[i * share + first : i * share + first + group, columns] = (
                            mine * factor[i]
                        ).astype(weighted.dtype)

    load_cotangent.wait()
    rim_copy(0).wait_recv()
    came = jnp.where(me > 0, rims[2], 0.0)
    padded = jnp.concatenate([jnp.zeros((LANES - 8, came.shape[1]), jnp.float32), came], axis=0)
    before[...] = jnp.zeros_like(before)
    before[:, length - LANES :] = padded.T

    @each_group
    def _(rows):
        shifted = delayed_by(gates[rows, :].astype(jnp.float32), before[rows, :])
        short = conv(gate_taps(rows), shifted)
        short_gates[rows, :] = short
        long_here[rows, :] = (cotangent[rows, :].astype(jnp.float32) * short).astype(long_here.dtype)

    start_in(1)
    fields[1, me] = long_here[rows_of(b, s), :]

    load_filters.wait()
    each_batch(lambda bt: side_copy(1, bt, bt).wait_recv())
    each_batch(lambda bt: side_copy(0, bt, bt).wait_recv())
    for bt in range(batch):
        flat = filters_landed[bt].astype(jnp.float32).reshape(share * blocks, freqs)
        for half in range(freqs // LANES):
            lanes = slice(half * LANES, (half + 1) * LANES)
            unpacked[half] = flat[:, lanes]
            for p in range(blocks):
                filters[bt, p, :, lanes] = unpacked[half, pl.ds(p, share, stride=blocks), :]

    load_values.wait()
    wait_in(0)

    @each_chunk
    def _(d, rows, columns):
        short_values[rows, columns] = conv(value_taps, delays(d)).astype(short_values.dtype)

    load_cas.wait()
    times_table(short_values, wide)
    mix(True)
    times_table(weighted, filtered)

    @each_chunk
    def _(d, rows, columns):
        short = short_values[rows, columns].astype(jnp.float32)
        inner = filtered[rows, columns].astype(jnp.float32) + skip * short
        out_fields[0, d] = inner.astype(out_fields.dtype)

    start_out(0)

    wait_in(1)

    @each_chunk
    def _(d, rows, columns):
        grad_long[rows, columns] = fields[1, d]

    times_table(grad_long, wide)
    mix(False)
    each_batch(lambda bt: side_copy(2, bt, b).start())
    spectrum_landed[:, batch_rows(b), :] = out_spectrum[b]
    times_table(weighted, filtered)

    @each_chunk
    def _(d, rows, columns):
        grads = skip * grad_long[rows, columns].astype(jnp.float32)
        gradient[d] = grads + filtered[rows, columns].astype(jnp.float32)

    @each_chunk
    def _(d, rows, columns):
        out_fields[1, d] = conv(value_taps, advances(d)).astype(out_fields.dtype)

    start_out(1)

    @each_chunk
    def _(d, rows, columns):
        shifted = delays(d)
        grads = gradient[d]
        for k in range(3):
            totals[k] += grads * shifted[k]
        totals[3] += grad_long[rows, columns].astype(jnp.float32) * short_values[
            rows, columns
        ].astype(jnp.float32)

    column = lax.broadcasted_iota(jnp.int32, (share, LANES), 1)

    def in_columns(columns):
        result = jnp.zeros((share, LANES), jnp.float32)
        for k, value in enumerate(columns):
            result = jnp.where(column == k, jnp.sum(value, axis=1, keepdims=True), result)
        return result

    own = in_columns([totals[k] for k in range(4)])
    own = jnp.concatenate([own, jnp.zeros((LANES - share, LANES), jnp.float32)], axis=0)
    sums[b] = own.T[:8, :]
    each_batch(lambda bt: side_copy(3, bt, b).start())

    each_other(lambda peer, bt, st: out_copy(0, peer, bt, st, peer).wait_recv())

    @each_group
    def _(rows):
        inner = inner_here[rows, :].astype(jnp.float32)
        mixed[rows, :] = (short_gates[rows, :] * inner).astype(mixed.dtype)
        grads = cotangent[rows, :].astype(jnp.float32) * inner
        gates_gradient[rows, :] = grads
        shifted = delayed_by(gates[rows, :].astype(jnp.float32), before[rows, :])
        line[rows, :] = in_columns([grads * shifted[k] for k in range(3)])

    rims[1] = gates_gradient[:, :LANES].T[:8, :]
    rim_copy(1).start()
    turned = line[...].T[:8, :]
    for st in range(seq):
        parts[0, st] = turned[:, st * width : (st + 1) * width]
    each_seq(lambda st: part_copy(st, s).start())
    parts[1, s] = parts[0, s]
    rim_copy(1).wait_recv()
    came = jnp.where(me < count - 1, rims[3], 0.0)
    padded = jnp.concatenate([came, jnp.zeros((LANES - 8, came.shape[1]), jnp.float32)], axis=0)
    after[...] = jnp.zeros_like(after)
    after[:, :LANES] = padded.T

    @each_group
    def _(rows):
        shifted = advanced_by(gates_gradient[rows, :], after[rows, :])
        grad_gates[rows, :] = conv(gate_taps(rows), shifted).astype(grad_gates.dtype)

    each_seq(lambda st: part_copy(st, st).wait_recv())
    total = parts[1, 0]
    for st in range(1, seq):
        total = total + parts[1, st]
    batch_parts[b] = total
    each_batch(lambda bt: side_copy(4, bt, b).start())
    each_batch(lambda bt: side_copy(4, bt, bt).wait_recv())
    total = batch_parts[0]
    for bt in range(1, batch):
        total = total + batch_parts[bt]
    gate_sums[...] = total[:3, :]

    each_batch(lambda bt: side_copy(2, bt, bt).wait_recv())
    for p in range(blocks):
        for half in range(freqs // LANES):
            lanes = slice(half * LANES, (half + 1) * LANES)
            grad_spectrum[half, pl.ds(p, width, stride=blocks), :] = spectrum_landed[p, :, lanes].astype(jnp.float32)
    each_batch(lambda bt: side_copy(3, bt, bt).wait_recv())
    total = jnp.concatenate([sums[bt, :, :share] for bt in range(batch)], axis=1)
    value_sums[...] = total[:3, :]
    skip_sums[...] = total[3:4, :]

    each_seq(lambda st: part_copy(st, s).wait_send())
    for n in range(2):
        rim_copy(n).wait_send()
        each_other(lambda peer, bt, st: in_copy(n, peer, bt, st, me).wait_send())
        each_other(lambda peer, bt, st: out_copy(n, peer, bt, st, me).wait_send())
    for n in range(5):
        each_batch(lambda bt: side_copy(n, bt, b).wait_send())
    each_other(lambda peer, bt, st: out_copy(1, peer, bt, st, peer).wait_recv())


def per_device_kernel(
    values, gates, cotangent, taps_values, taps_gates, skip_gain, twiddle, mixing, spectrum
):
    batch, seq = lax.axis_size("batch"), lax.axis_size("seq")
    count = batch * seq
    channels, length = values.shape
    share = channels // count
    blocks, block = mixing.shape[0], twiddle.shape[1]
    freqs = block // batch
    vmem = pl.BlockSpec(memory_space=pltpu.VMEM)
    hbm = pl.BlockSpec(memory_space=pl.ANY)
    smem = pl.BlockSpec(memory_space=pltpu.SMEM)
    field = jax.ShapeDtypeStruct((channels, length), jnp.bfloat16)
    rows = blocks * share
    mixed, grad_values, grad_gates, grad_spectrum, value_sums, gate_sums, skip_sums = pl.pallas_call(
        functools.partial(whole_sequences, batch, seq),
        out_shape=[
            field, field, field,
            jax.ShapeDtypeStruct((freqs // LANES, blocks * channels // seq, LANES), jnp.float32),
            jax.ShapeDtypeStruct((3, channels // seq), jnp.float32),
            jax.ShapeDtypeStruct((3, channels // seq), jnp.float32),
            jax.ShapeDtypeStruct((1, channels // seq), jnp.float32),
        ],
        in_specs=[hbm, hbm, hbm, hbm, vmem, smem, vmem, vmem, vmem, hbm],
        out_specs=[vmem] * 7,
        scratch_shapes=[
            pltpu.VMEM((channels, length), jnp.bfloat16),
            pltpu.VMEM((channels, length), jnp.bfloat16),
            pltpu.VMEM((block, block), jnp.bfloat16),
            pltpu.VMEM((channels, LANES), jnp.float32),
            pltpu.VMEM((LANES, channels), jnp.float32),
            pltpu.VMEM((batch, share, blocks, freqs), jnp.bfloat16),
            pltpu.VMEM((freqs // LANES, share * blocks, LANES), jnp.float32),
            pltpu.VMEM((blocks, channels // seq, freqs), jnp.bfloat16),
            pltpu.VMEM((batch, 8, LANES), jnp.float32),
            pltpu.VMEM((2, count, share, length), jnp.bfloat16),
            pltpu.VMEM((batch, blocks, share, freqs), jnp.float32),
            pltpu.VMEM((batch, blocks // batch, block), jnp.float32),
            pltpu.VMEM((rows, block), jnp.bfloat16),
            pltpu.VMEM((rows, block), jnp.bfloat16),
            pltpu.VMEM((rows, block), jnp.float32),
            pltpu.VMEM((rows, block), jnp.bfloat16),
            pltpu.VMEM((rows, block), jnp.float32),
            pltpu.VMEM((rows, block), jnp.bfloat16),
            pltpu.VMEM((count, share, length), jnp.float32),
            pltpu.VMEM((2, count, share, length), jnp.bfloat16),
            pltpu.VMEM((batch, blocks, share, freqs), jnp.bfloat16),
            pltpu.VMEM((4, share, length), jnp.float32),
            pltpu.VMEM((channels, length), jnp.float32),
            pltpu.VMEM((channels, length), jnp.bfloat16),
            pltpu.VMEM((channels, length), jnp.bfloat16),
            pltpu.VMEM((channels, length), jnp.float32),
            pltpu.VMEM((channels, length), jnp.float32),
            pltpu.VMEM((channels, length), jnp.float32),
            pltpu.VMEM((4, 8, channels), jnp.float32),
            pltpu.VMEM((channels, LANES), jnp.float32),
            pltpu.VMEM((2, seq, 8, channels // seq), jnp.float32),
            pltpu.VMEM((batch, 8, channels // seq), jnp.float32),
            pltpu.SemaphoreType.DMA((2, count)),
            pltpu.SemaphoreType.DMA((2, count)),
            pltpu.SemaphoreType.DMA((2, count)),
            pltpu.SemaphoreType.DMA((2, count)),
            pltpu.SemaphoreType.DMA((5, batch)),
            pltpu.SemaphoreType.DMA((5, batch)),
            pltpu.SemaphoreType.DMA((2,)),
            pltpu.SemaphoreType.DMA((2,)),
            pltpu.SemaphoreType.DMA((seq,)),
            pltpu.SemaphoreType.DMA((seq,)),
            pltpu.SemaphoreType.DMA((5,)),
        ],
        compiler_params=pltpu.CompilerParams(
            collective_id=0, has_side_effects=True, vmem_limit_bytes=56 * 2**20
        ),
    )(
        values, gates, cotangent, spectrum, twiddle, mixing, taps_values, taps_gates,
        skip_gain[None], cas_table(block),
    )
    grad_spectrum = grad_spectrum.reshape(-1, channels // seq, blocks, LANES)
    grad_spectrum = jnp.concatenate(list(grad_spectrum), axis=2)
    return (
        mixed, grad_values, grad_gates, grad_spectrum, value_sums, gate_sums, skip_sums[0]
    )


def per_device(values, *rest):
    twiddle, mixing = rest[5], rest[6]
    batch = lax.axis_size("batch")
    count = batch * lax.axis_size("seq")
    channels, length = values.shape
    block = twiddle.shape[1]
    fits = (
        channels % (count * 16) == 0
        and length % LANES == 0
        and channels % (lax.axis_size("seq") * LANES) == 0
        and block % length == 0
        and block % (batch * LANES) == 0
        and mixing.shape[0] % batch == 0
        and mixing.shape[0] % 8 == 0
        and channels // count <= LANES
    )
    return (per_device_kernel if fits else per_device_plain)(values, *rest)


def solution(mesh):
    spread = P(None, AXES)
    in_specs = (
        spread, spread, spread, P(), P(), P(), P("batch", None), P(), P("seq", None, "batch")
    )
    out_specs = (
        spread, spread, spread, P("seq", None, "batch"), P(None, "seq"), P(None, "seq"), P("seq")
    )
    return jax.shard_map(
        per_device, mesh=mesh, in_specs=in_specs, out_specs=out_specs, check_vma=False
    )
```

```python
import functools
import math

import jax
import jax.numpy as jnp
import numpy as np
from jax import lax
from jax.experimental import pallas as pl
from jax.experimental.pallas import tpu as pltpu
from jax.sharding import PartitionSpec as P

AXES = ("batch", "seq")


def cas_table(block):
    angles = np.arange(block, dtype=np.float32) * np.float32(2.0 * math.pi / block)
    entries = (np.cos(angles) + np.sin(angles)) / np.float32(math.sqrt(block))
    indices = np.arange(block)
    return jnp.asarray(entries.astype(jnp.bfloat16)[indices[:, None] * indices[None, :] % block])


def delayed(field, steps):
    return jnp.pad(field, ((0, 0), (steps, 0)))[:, : field.shape[1]]


def advanced(field, steps):
    return jnp.pad(field, ((0, 0), (0, steps)))[:, steps:]


def short_conv(field, taps, shift):
    return (
        taps[0][:, None] * field
        + taps[1][:, None] * shift(field, 1)
        + taps[2][:, None] * shift(field, 2)
    )


def tap_sums(gradient, field):
    return jnp.stack([jnp.sum(gradient * delayed(field, s), axis=1) for s in range(3)])


def per_device_plain(
    values, gates, cotangent, taps_values, taps_gates, skip_gain, twiddle, mixing, spectrum
):
    block = twiddle.shape[1]
    cas = cas_table(block)
    batch, seq = lax.axis_size("batch"), lax.axis_size("seq")
    share = values.shape[0] // (batch * seq)
    b, s = lax.axis_index("batch"), lax.axis_index("seq")
    start = (s * batch + b) * share
    stacked = jnp.stack([values, gates, cotangent])
    length_dev = values.shape[1]
    stacked = stacked.reshape(3, seq, batch, share, length_dev).transpose(2, 1, 0, 3, 4)
    stacked = stacked.reshape(batch * seq, 3, share, length_dev)
    whole = lax.all_to_all(stacked, AXES, split_axis=0, concat_axis=0, tiled=True)
    whole = whole.transpose(1, 2, 0, 3).reshape(3, share, -1)
    filters = lax.all_to_all(spectrum, "batch", split_axis=0, concat_axis=2, tiled=True)
    filters = filters.astype(jnp.float32)
    factors = lax.all_gather(twiddle, "batch", axis=0, tiled=True)
    params = jnp.concatenate([taps_values, taps_gates, skip_gain[None]], axis=0)
    params = lax.dynamic_slice_in_dim(params, start, share, 1)
    value_taps, gate_taps, skip = params[:3], params[3:6], params[6][:, None]
    field, gate, cot = (whole[n].astype(jnp.float32) for n in range(3))
    short_values = short_conv(field, value_taps, delayed).astype(jnp.bfloat16)
    short_gates = short_conv(gate, gate_taps, delayed)
    grad_long = (cot * short_gates).astype(jnp.bfloat16)

    def transform(source):
        sums = jnp.dot(source.reshape(-1, block), cas, preferred_element_type=jnp.float32)
        sums = sums.reshape(share, -1, block) * factors
        return jnp.einsum("pi,cik->cpk", mixing, sums, precision=lax.Precision.HIGHEST)

    def back(spectra):
        mixed = jnp.einsum("pi,cpk->cik", mixing, spectra, precision=lax.Precision.HIGHEST)
        weighted = (mixed * factors).astype(jnp.bfloat16)
        result = jnp.dot(weighted.reshape(-1, block), cas, preferred_element_type=jnp.float32)
        return result.reshape(share, -1).astype(jnp.bfloat16).astype(jnp.float32)

    spectra_values, spectra_grads = transform(short_values), transform(grad_long)
    long_values, back_grads = back(spectra_values * filters), back(spectra_grads * filters)
    grad_spectrum = (spectra_values * spectra_grads).astype(jnp.bfloat16)
    grad_spectrum = lax.all_to_all(grad_spectrum, "batch", split_axis=2, concat_axis=0, tiled=True)
    short_f32 = short_values.astype(jnp.float32)
    long_f32 = grad_long.astype(jnp.float32)
    inner = long_values + skip * short_f32
    grad_short_gates = cot * inner
    grad_short_values = skip * long_f32 + back_grads
    outs = jnp.stack([
        (short_gates * inner).astype(jnp.bfloat16),
        short_conv(grad_short_values, value_taps, advanced).astype(jnp.bfloat16),
        short_conv(grad_short_gates, gate_taps, advanced).astype(jnp.bfloat16),
    ])
    outs = outs.reshape(3, share, batch * seq, length_dev).transpose(2, 0, 1, 3)
    outs = lax.all_to_all(outs, AXES, split_axis=0, concat_axis=0, tiled=True)
    outs = outs.reshape(batch, seq, 3, share, length_dev).transpose(2, 1, 0, 3, 4)
    outs = outs.reshape(3, -1, length_dev)
    sums = jnp.concatenate([
        tap_sums(grad_short_values, field),
        tap_sums(grad_short_gates, gate),
        jnp.sum(long_f32 * short_f32, axis=1)[None],
    ])
    sums = lax.all_gather(sums, "batch", axis=1, tiled=True)
    return (
        outs[0], outs[1], outs[2], grad_spectrum.astype(jnp.float32), sums[:3], sums[3:6], sums[6]
    )


LANES = 128
MESH = pl.DeviceIdType.MESH


def whole_sequences(
    batch, seq,
    values, gates_in, cotangent_in, spectrum, twiddle, mixing, value_taps_in, gate_taps_in, skip_in, cas_in,
    mixed, grad_values, grad_gates, grad_spectrum, value_sums, gate_sums, skip_sums,
    gates, cotangent, cas, params, turned_params, filters_landed, unpacked, spectrum_landed, sums, turned_spectrum,
    fields, filters, factors, short_values, grad_long, wide, weighted,
    spectra, filtered, gradient, out_fields, out_spectrum, totals,
    short_gates, long_here, inner_here, gates_gradient, before, after, rims, line, parts, batch_parts,
    in_send, in_recv, out_send, out_recv, side_send, side_recv, rim_send, rim_recv,
    part_send, part_recv, local,
):
    b, s = lax.axis_index("batch"), lax.axis_index("seq")
    count = batch * seq
    me = b * seq + s
    share, length = fields.shape[2], fields.shape[3]
    block = cas.shape[0]
    blocks = short_values.shape[0] // share
    per_block = block // length
    freqs = block // batch

    def rows_of(bt, st):
        return pl.ds(pl.multiple_of((st * batch + bt) * share, share), share)

    def batch_rows(bt):
        return pl.ds(pl.multiple_of(bt * share, share), share)

    def other(step):
        peer = lax.rem(me + step, count)
        return peer, lax.div(peer, seq), lax.rem(peer, seq)

    def each_other(body):
        @pl.loop(1, count)
        def _(step):
            body(*other(step))

    def each_batch(body):
        for step in range(1, batch):
            body(lax.rem(b + step, batch))

    load_gates = pltpu.make_async_copy(gates_in, gates, local.at[0])
    load_cotangent = pltpu.make_async_copy(cotangent_in, cotangent, local.at[1])
    load_cas = pltpu.make_async_copy(cas_in, cas, local.at[2])
    load_values = pltpu.make_async_copy(values.at[rows_of(b, s), :], fields.at[0, me], local.at[3])
    load_filters = pltpu.make_async_copy(
        spectrum.at[batch_rows(b)], filters_landed.at[b], local.at[4]
    )

    barrier = pltpu.get_barrier_semaphore()
    each_other(lambda peer, bt, st: pl.semaphore_signal(
        barrier, inc=1, device_id=(bt, st), device_id_type=MESH))
    load_gates.start()
    load_cotangent.start()
    load_values.start()
    load_cas.start()
    load_filters.start()
    turned_params[...] = jnp.zeros_like(turned_params)
    turned_params[0:3, :] = value_taps_in[...]
    turned_params[3:6, :] = gate_taps_in[...]
    turned_params[6:7, :] = skip_in[...]
    params[...] = turned_params[...].T
    load_gates.wait()
    rims[0] = gates[:, length - LANES :].astype(jnp.float32).T[LANES - 8 :, :]
    pl.semaphore_wait(barrier, count - 1)

    def in_copy(n, peer, bt, st):
        return pltpu.make_async_remote_copy(
            src_ref=(values, long_here)[n].at[rows_of(bt, st), :],
            dst_ref=fields.at[n, me],
            send_sem=in_send.at[n],
            recv_sem=in_recv.at[n],
            device_id=(bt, st),
            device_id_type=MESH,
        )

    def out_copy(n, peer, bt, st):
        return pltpu.make_async_remote_copy(
            src_ref=out_fields.at[n, peer],
            dst_ref=(inner_here, grad_values)[n].at[rows_of(b, s), :],
            send_sem=out_send.at[n],
            recv_sem=out_recv.at[n],
            device_id=(bt, st),
            device_id_type=MESH,
        )

    def side_copy(n, bt, slot):
        source = (
            spectrum.at[batch_rows(bt)], twiddle, out_spectrum.at[bt], sums.at[b], batch_parts.at[b]
        )[n]
        target = (
            filters_landed.at[b], factors.at[b], spectrum_landed.at[:, batch_rows(b), :], sums.at[b], batch_parts.at[b]
        )[n]
        return pltpu.make_async_remote_copy(
            src_ref=source,
            dst_ref=target,
            send_sem=side_send.at[n, bt],
            recv_sem=side_recv.at[n, slot],
            device_id=(bt, s),
            device_id_type=MESH,
        )

    def rim_copy(n):
        peer = lax.rem(me + (1, count - 1)[n], count)
        return pltpu.make_async_remote_copy(
            src_ref=rims.at[n],
            dst_ref=rims.at[2 + n],
            send_sem=rim_send.at[n],
            recv_sem=rim_recv.at[n],
            device_id=(lax.div(peer, seq), lax.rem(peer, seq)),
            device_id_type=MESH,
        )

    width = values.shape[0] // seq

    def part_copy(st, slot):
        return pltpu.make_async_remote_copy(
            src_ref=parts.at[0, st],
            dst_ref=parts.at[1, s],
            send_sem=part_send.at[st],
            recv_sem=part_recv.at[slot],
            device_id=(b, st),
            device_id_type=MESH,
        )

    def each_seq(body):
        for step in range(1, seq):
            body(lax.rem(s + step, seq))

    def start_in(n):
        each_other(lambda peer, bt, st: in_copy(n, peer, bt, st).start())

    def wait_all(buffer, semaphore):
        pieces = buffer.at[pl.ds(0, count - 1)]
        pltpu.make_async_copy(pieces, pieces, semaphore).wait()

    def wait_in(n):
        wait_all(fields.at[n], in_recv.at[n])

    def start_out(n):
        each_other(lambda peer, bt, st: out_copy(n, peer, bt, st).start())
        (inner_here, grad_values)[n][rows_of(b, s), :] = out_fields[n, me]

    rim_copy(0).start()
    start_in(0)
    each_batch(lambda bt: side_copy(1, bt, b).start())
    each_batch(lambda bt: side_copy(0, bt, b).start())
    factors[b] = twiddle[...]
    totals[...] = jnp.zeros_like(totals)

    lane = lax.broadcasted_iota(jnp.int32, (share, length), 1)
    mine_rows = rows_of(b, s)
    value_taps = [params[mine_rows, n : n + 1] for n in range(3)]
    skip = params[mine_rows, 6:7]
    matrix = [[mixing[p, i] for i in range(blocks)] for p in range(blocks)]

    def delayed_by(now, earlier):
        return [now] + [
            jnp.where(lane < k, pltpu.roll(earlier, k, 1), pltpu.roll(now, k, 1)) for k in (1, 2)
        ]

    def advanced_by(now, later):
        return [now] + [
            jnp.where(
                lane >= length - k, pltpu.roll(later, length - k, 1), pltpu.roll(now, length - k, 1)
            )
            for k in (1, 2)
        ]

    def delays(d):
        now = fields[0, d].astype(jnp.float32)
        earlier = fields[0, jnp.maximum(d - 1, 0)].astype(jnp.float32)
        return delayed_by(now, jnp.where(d > 0, earlier, 0.0))

    def advances(d):
        later = jnp.where(d < count - 1, gradient[jnp.minimum(d + 1, count - 1)], 0.0)
        return advanced_by(gradient[d], later)

    def gate_taps(rows):
        return [params[rows, n : n + 1] for n in range(3, 6)]

    def each_group(body):
        @pl.loop(0, count)
        def _(g):
            body(pl.ds(pl.multiple_of(g * share, share), share))

    def conv(taps, shifted):
        return taps[0] * shifted[0] + taps[1] * shifted[1] + taps[2] * shifted[2]

    def each_chunk(body):
        @pl.loop(0, blocks)
        def _(i):
            for q in range(per_block):
                rows = pl.ds(pl.multiple_of(i * share, share), share)
                body(i * per_block + q, rows, slice(q * length, (q + 1) * length))

    def times_table(source, target):
        tile = min(256, block)

        @pl.loop(0, block // tile)
        def _(at):
            columns = pl.ds(pl.multiple_of(at * tile, tile), tile)
            product = jnp.dot(source[...], cas[:, columns], preferred_element_type=jnp.float32)
            target[:, columns] = product.astype(target.dtype)

    def mix(of_values):
        group = 16

        @pl.loop(0, batch)
        def _(kt):
            for inside in range(0, freqs, LANES):
                columns = pl.ds(pl.multiple_of(kt * freqs + inside, LANES), LANES)
                part = slice(inside, inside + LANES)
                per_batch = blocks // batch
                factor = [
                    factors[i // per_batch, i % per_batch : i % per_batch + 1, columns]
                    for i in range(blocks)
                ]
                for first in range(0, share, group):
                    rows = slice(first, first + group)
                    sums_in = [
                        wide[i * share + first : i * share + first + group, columns] * factor[i]
                        for i in range(blocks)
                    ]
                    products = []
                    for p in range(blocks):
                        mine = matrix[p][0] * sums_in[0]
                        for i in range(1, blocks):
                            mine = mine + matrix[p][i] * sums_in[i]
                        at = slice(p * share + first, p * share + first + group)
                        if of_values:
                            spectra[at, columns] = mine
                        else:
                            out_spectrum[kt, p, rows, part] = (
                                spectra[at, columns] * mine
                            ).astype(out_spectrum.dtype)
                        products.append(mine * filters[kt, p, rows, part])
                    for i in range(blocks):
                        mine = matrix[0][i] * products[0]
                        for p in range(1, blocks):
                            mine = mine + matrix[p][i] * products[p]
                        weighted[i * share + first : i * share + first + group, columns] = (
                            mine * factor[i]
                        ).astype(weighted.dtype)

    load_cotangent.wait()
    rim_copy(0).wait_recv()
    came = jnp.where(me > 0, rims[2], 0.0)
    padded = jnp.concatenate([jnp.zeros((LANES - 8, came.shape[1]), jnp.float32), came], axis=0)
    before[...] = jnp.zeros_like(before)
    before[:, length - LANES :] = padded.T

    @each_group
    def _(rows):
        shifted = delayed_by(gates[rows, :].astype(jnp.float32), before[rows, :])
        short = conv(gate_taps(rows), shifted)
        short_gates[rows, :] = short
        long_here[rows, :] = (cotangent[rows, :].astype(jnp.float32) * short).astype(long_here.dtype)

    start_in(1)
    fields[1, me] = long_here[rows_of(b, s), :]

    load_filters.wait()
    each_batch(lambda bt: side_copy(1, bt, bt).wait_recv())
    each_batch(lambda bt: side_copy(0, bt, bt).wait_recv())
    for bt in range(batch):
        flat = filters_landed[bt].astype(jnp.float32).reshape(share * blocks, freqs)
        for half in range(freqs // LANES):
            lanes = slice(half * LANES, (half + 1) * LANES)
            unpacked[half] = flat[:, lanes]
            for p in range(blocks):
                filters[bt, p, :, lanes] = unpacked[half, pl.ds(p, share, stride=blocks), :]

    load_values.wait()
    wait_in(0)

    @each_chunk
    def _(d, rows, columns):
        short_values[rows, columns] = conv(value_taps, delays(d)).astype(short_values.dtype)

    load_cas.wait()
    times_table(short_values, wide)
    mix(True)
    times_table(weighted, filtered)

    @each_chunk
    def _(d, rows, columns):
        short = short_values[rows, columns].astype(jnp.float32)
        inner = filtered[rows, columns].astype(jnp.float32) + skip * short
        out_fields[0, d] = inner.astype(out_fields.dtype)

    start_out(0)

    wait_in(1)

    @each_chunk
    def _(d, rows, columns):
        grad_long[rows, columns] = fields[1, d]

    times_table(grad_long, wide)
    mix(False)
    each_batch(lambda bt: side_copy(2, bt, b).start())
    spectrum_landed[:, batch_rows(b), :] = out_spectrum[b]
    times_table(weighted, filtered)

    @each_chunk
    def _(d, rows, columns):
        grads = skip * grad_long[rows, columns].astype(jnp.float32)
        gradient[d] = grads + filtered[rows, columns].astype(jnp.float32)

    @each_chunk
    def _(d, rows, columns):
        out_fields[1, d] = conv(value_taps, advances(d)).astype(out_fields.dtype)

    start_out(1)

    column = lax.broadcasted_iota(jnp.int32, (share, LANES), 1)

    def in_columns(columns):
        result = jnp.zeros((share, LANES), jnp.float32)
        for k, value in enumerate(columns):
            result = jnp.where(column == k, jnp.sum(value, axis=1, keepdims=True), result)
        return result

    wait_all(out_fields.at[0], out_recv.at[0])

    @each_group
    def _(rows):
        inner = inner_here[rows, :].astype(jnp.float32)
        mixed[rows, :] = (short_gates[rows, :] * inner).astype(mixed.dtype)
        grads = cotangent[rows, :].astype(jnp.float32) * inner
        gates_gradient[rows, :] = grads
        shifted = delayed_by(gates[rows, :].astype(jnp.float32), before[rows, :])
        line[rows, :] = in_columns([grads * shifted[k] for k in range(3)])

    rims[1] = gates_gradient[:, :LANES].T[:8, :]
    rim_copy(1).start()
    turned = line[...].T[:8, :]
    for st in range(seq):
        parts[0, st] = turned[:, st * width : (st + 1) * width]
    each_seq(lambda st: part_copy(st, s).start())
    parts[1, s] = parts[0, s]
    @each_chunk
    def _(d, rows, columns):
        shifted = delays(d)
        grads = gradient[d]
        for k in range(3):
            totals[k] += grads * shifted[k]
        totals[3] += grad_long[rows, columns].astype(jnp.float32) * short_values[
            rows, columns
        ].astype(jnp.float32)

    own = in_columns([totals[k] for k in range(4)])
    own = jnp.concatenate([own, jnp.zeros((LANES - share, LANES), jnp.float32)], axis=0)
    sums[b] = own.T[:8, :]
    each_batch(lambda bt: side_copy(3, bt, b).start())

    rim_copy(1).wait_recv()
    came = jnp.where(me < count - 1, rims[3], 0.0)
    padded = jnp.concatenate([came, jnp.zeros((LANES - 8, came.shape[1]), jnp.float32)], axis=0)
    after[...] = jnp.zeros_like(after)
    after[:, :LANES] = padded.T

    @each_group
    def _(rows):
        shifted = advanced_by(gates_gradient[rows, :], after[rows, :])
        grad_gates[rows, :] = conv(gate_taps(rows), shifted).astype(grad_gates.dtype)

    each_batch(lambda bt: side_copy(2, bt, bt).wait_recv())
    for p in range(blocks):
        for half in range(freqs // LANES):
            lanes = slice(half * LANES, (half + 1) * LANES)
            turned_spectrum[half, pl.ds(p, width, stride=blocks), :] = spectrum_landed[p, :, lanes].astype(jnp.float32)
    for half in range(freqs // LANES):
        grad_spectrum[:, half * LANES : (half + 1) * LANES] = turned_spectrum[half]
    each_seq(lambda st: part_copy(st, st).wait_recv())
    total = parts[1, 0]
    for st in range(1, seq):
        total = total + parts[1, st]
    batch_parts[b] = total
    each_batch(lambda bt: side_copy(4, bt, b).start())
    each_batch(lambda bt: side_copy(4, bt, bt).wait_recv())
    total = batch_parts[0]
    for bt in range(1, batch):
        total = total + batch_parts[bt]
    gate_sums[...] = total[:3, :]

    each_batch(lambda bt: side_copy(3, bt, bt).wait_recv())
    total = jnp.concatenate([sums[bt, :, :share] for bt in range(batch)], axis=1)
    value_sums[...] = total[:3, :]
    skip_sums[...] = total[3:4, :]

    each_seq(lambda st: part_copy(st, s).wait_send())
    for n in range(2):
        rim_copy(n).wait_send()
        wait_all(fields.at[n], in_send.at[n])
        wait_all(out_fields.at[n], out_send.at[n])
    for n in range(5):
        each_batch(lambda bt: side_copy(n, bt, b).wait_send())
    wait_all(out_fields.at[1], out_recv.at[1])


def per_device_kernel(
    values, gates, cotangent, taps_values, taps_gates, skip_gain, twiddle, mixing, spectrum
):
    batch, seq = lax.axis_size("batch"), lax.axis_size("seq")
    count = batch * seq
    channels, length = values.shape
    share = channels // count
    blocks, block = mixing.shape[0], twiddle.shape[1]
    freqs = block // batch
    vmem = pl.BlockSpec(memory_space=pltpu.VMEM)
    hbm = pl.BlockSpec(memory_space=pl.ANY)
    smem = pl.BlockSpec(memory_space=pltpu.SMEM)
    field = jax.ShapeDtypeStruct((channels, length), jnp.bfloat16)
    rows = blocks * share
    mixed, grad_values, grad_gates, grad_spectrum, value_sums, gate_sums, skip_sums = pl.pallas_call(
        functools.partial(whole_sequences, batch, seq),
        out_shape=[
            field, field, field,
            jax.ShapeDtypeStruct((blocks * channels // seq, freqs), jnp.float32),
            jax.ShapeDtypeStruct((3, channels // seq), jnp.float32),
            jax.ShapeDtypeStruct((3, channels // seq), jnp.float32),
            jax.ShapeDtypeStruct((1, channels // seq), jnp.float32),
        ],
        in_specs=[hbm, hbm, hbm, hbm, vmem, smem, vmem, vmem, vmem, hbm],
        out_specs=[vmem] * 7,
        scratch_shapes=[
            pltpu.VMEM((channels, length), jnp.bfloat16),
            pltpu.VMEM((channels, length), jnp.bfloat16),
            pltpu.VMEM((block, block), jnp.bfloat16),
            pltpu.VMEM((channels, LANES), jnp.float32),
            pltpu.VMEM((LANES, channels), jnp.float32),
            pltpu.VMEM((batch, share, blocks, freqs), jnp.bfloat16),
            pltpu.VMEM((freqs // LANES, share * blocks, LANES), jnp.float32),
            pltpu.VMEM((blocks, channels // seq, freqs), jnp.bfloat16),
            pltpu.VMEM((batch, 8, LANES), jnp.float32),
            pltpu.VMEM((freqs // LANES, blocks * channels // seq, LANES), jnp.float32),
            pltpu.VMEM((2, count, share, length), jnp.bfloat16),
            pltpu.VMEM((batch, blocks, share, freqs), jnp.float32),
            pltpu.VMEM((batch, blocks // batch, block), jnp.float32),
            pltpu.VMEM((rows, block), jnp.bfloat16),
            pltpu.VMEM((rows, block), jnp.bfloat16),
            pltpu.VMEM((rows, block), jnp.float32),
            pltpu.VMEM((rows, block), jnp.bfloat16),
            pltpu.VMEM((rows, block), jnp.float32),
            pltpu.VMEM((rows, block), jnp.bfloat16),
            pltpu.VMEM((count, share, length), jnp.float32),
            pltpu.VMEM((2, count, share, length), jnp.bfloat16),
            pltpu.VMEM((batch, blocks, share, freqs), jnp.bfloat16),
            pltpu.VMEM((4, share, length), jnp.float32),
            pltpu.VMEM((channels, length), jnp.float32),
            pltpu.VMEM((channels, length), jnp.bfloat16),
            pltpu.VMEM((channels, length), jnp.bfloat16),
            pltpu.VMEM((channels, length), jnp.float32),
            pltpu.VMEM((channels, length), jnp.float32),
            pltpu.VMEM((channels, length), jnp.float32),
            pltpu.VMEM((4, 8, channels), jnp.float32),
            pltpu.VMEM((channels, LANES), jnp.float32),
            pltpu.VMEM((2, seq, 8, channels // seq), jnp.float32),
            pltpu.VMEM((batch, 8, channels // seq), jnp.float32),
            pltpu.SemaphoreType.DMA((2,)),
            pltpu.SemaphoreType.DMA((2,)),
            pltpu.SemaphoreType.DMA((2,)),
            pltpu.SemaphoreType.DMA((2,)),
            pltpu.SemaphoreType.DMA((5, batch)),
            pltpu.SemaphoreType.DMA((5, batch)),
            pltpu.SemaphoreType.DMA((2,)),
            pltpu.SemaphoreType.DMA((2,)),
            pltpu.SemaphoreType.DMA((seq,)),
            pltpu.SemaphoreType.DMA((seq,)),
            pltpu.SemaphoreType.DMA((5,)),
        ],
        compiler_params=pltpu.CompilerParams(
            collective_id=0, has_side_effects=True, vmem_limit_bytes=56 * 2**20
        ),
    )(
        values, gates, cotangent, spectrum, twiddle, mixing, taps_values, taps_gates,
        skip_gain[None], cas_table(block),
    )
    grad_spectrum = grad_spectrum.reshape(channels // seq, blocks, freqs)
    return (
        mixed, grad_values, grad_gates, grad_spectrum, value_sums, gate_sums, skip_sums[0]
    )


def per_device(values, *rest):
    twiddle, mixing = rest[5], rest[6]
    batch = lax.axis_size("batch")
    count = batch * lax.axis_size("seq")
    channels, length = values.shape
    block = twiddle.shape[1]
    fits = (
        channels % (count * 16) == 0
        and length % LANES == 0
        and channels % (lax.axis_size("seq") * LANES) == 0
        and block % length == 0
        and block % (batch * LANES) == 0
        and mixing.shape[0] % batch == 0
        and mixing.shape[0] % 8 == 0
        and channels // count <= LANES
    )
    return (per_device_kernel if fits else per_device_plain)(values, *rest)


def solution(mesh):
    spread = P(None, AXES)
    in_specs = (
        spread, spread, spread, P(), P(), P(), P("batch", None), P(), P("seq", None, "batch")
    )
    out_specs = (
        spread, spread, spread, P("seq", None, "batch"), P(None, "seq"), P(None, "seq"), P("seq")
    )
    return jax.shard_map(
        per_device, mesh=mesh, in_specs=in_specs, out_specs=out_specs, check_vma=False
    )
```

```python
import functools
import math

import jax
import jax.numpy as jnp
import numpy as np
from jax import lax
from jax.experimental import pallas as pl
from jax.experimental.pallas import tpu as pltpu
from jax.sharding import PartitionSpec as P

AXES = ("batch", "seq")


def cas_table(block):
    angles = np.arange(block, dtype=np.float32) * np.float32(2.0 * math.pi / block)
    entries = (np.cos(angles) + np.sin(angles)) / np.float32(math.sqrt(block))
    indices = np.arange(block)
    return jnp.asarray(entries.astype(jnp.bfloat16)[indices[:, None] * indices[None, :] % block])


def delayed(field, steps):
    return jnp.pad(field, ((0, 0), (steps, 0)))[:, : field.shape[1]]


def advanced(field, steps):
    return jnp.pad(field, ((0, 0), (0, steps)))[:, steps:]


def short_conv(field, taps, shift):
    return (
        taps[0][:, None] * field
        + taps[1][:, None] * shift(field, 1)
        + taps[2][:, None] * shift(field, 2)
    )


def tap_sums(gradient, field):
    return jnp.stack([jnp.sum(gradient * delayed(field, s), axis=1) for s in range(3)])


def per_device_plain(
    values, gates, cotangent, taps_values, taps_gates, skip_gain, twiddle, mixing, spectrum
):
    block = twiddle.shape[1]
    cas = cas_table(block)
    batch, seq = lax.axis_size("batch"), lax.axis_size("seq")
    share = values.shape[0] // (batch * seq)
    b, s = lax.axis_index("batch"), lax.axis_index("seq")
    start = (s * batch + b) * share
    stacked = jnp.stack([values, gates, cotangent])
    length_dev = values.shape[1]
    stacked = stacked.reshape(3, seq, batch, share, length_dev).transpose(2, 1, 0, 3, 4)
    stacked = stacked.reshape(batch * seq, 3, share, length_dev)
    whole = lax.all_to_all(stacked, AXES, split_axis=0, concat_axis=0, tiled=True)
    whole = whole.transpose(1, 2, 0, 3).reshape(3, share, -1)
    filters = lax.all_to_all(spectrum, "batch", split_axis=0, concat_axis=2, tiled=True)
    filters = filters.astype(jnp.float32)
    factors = lax.all_gather(twiddle, "batch", axis=0, tiled=True)
    params = jnp.concatenate([taps_values, taps_gates, skip_gain[None]], axis=0)
    params = lax.dynamic_slice_in_dim(params, start, share, 1)
    value_taps, gate_taps, skip = params[:3], params[3:6], params[6][:, None]
    field, gate, cot = (whole[n].astype(jnp.float32) for n in range(3))
    short_values = short_conv(field, value_taps, delayed).astype(jnp.bfloat16)
    short_gates = short_conv(gate, gate_taps, delayed)
    grad_long = (cot * short_gates).astype(jnp.bfloat16)

    def transform(source):
        sums = jnp.dot(source.reshape(-1, block), cas, preferred_element_type=jnp.float32)
        sums = sums.reshape(share, -1, block) * factors
        return jnp.einsum("pi,cik->cpk", mixing, sums, precision=lax.Precision.HIGHEST)

    def back(spectra):
        mixed = jnp.einsum("pi,cpk->cik", mixing, spectra, precision=lax.Precision.HIGHEST)
        weighted = (mixed * factors).astype(jnp.bfloat16)
        result = jnp.dot(weighted.reshape(-1, block), cas, preferred_element_type=jnp.float32)
        return result.reshape(share, -1).astype(jnp.bfloat16).astype(jnp.float32)

    spectra_values, spectra_grads = transform(short_values), transform(grad_long)
    long_values, back_grads = back(spectra_values * filters), back(spectra_grads * filters)
    grad_spectrum = (spectra_values * spectra_grads).astype(jnp.bfloat16)
    grad_spectrum = lax.all_to_all(grad_spectrum, "batch", split_axis=2, concat_axis=0, tiled=True)
    short_f32 = short_values.astype(jnp.float32)
    long_f32 = grad_long.astype(jnp.float32)
    inner = long_values + skip * short_f32
    grad_short_gates = cot * inner
    grad_short_values = skip * long_f32 + back_grads
    outs = jnp.stack([
        (short_gates * inner).astype(jnp.bfloat16),
        short_conv(grad_short_values, value_taps, advanced).astype(jnp.bfloat16),
        short_conv(grad_short_gates, gate_taps, advanced).astype(jnp.bfloat16),
    ])
    outs = outs.reshape(3, share, batch * seq, length_dev).transpose(2, 0, 1, 3)
    outs = lax.all_to_all(outs, AXES, split_axis=0, concat_axis=0, tiled=True)
    outs = outs.reshape(batch, seq, 3, share, length_dev).transpose(2, 1, 0, 3, 4)
    outs = outs.reshape(3, -1, length_dev)
    sums = jnp.concatenate([
        tap_sums(grad_short_values, field),
        tap_sums(grad_short_gates, gate),
        jnp.sum(long_f32 * short_f32, axis=1)[None],
    ])
    sums = lax.all_gather(sums, "batch", axis=1, tiled=True)
    return (
        outs[0], outs[1], outs[2], grad_spectrum.astype(jnp.float32), sums[:3], sums[3:6], sums[6]
    )


LANES = 128
MESH = pl.DeviceIdType.MESH


def whole_sequences(
    batch, seq,
    values, gates_in, cotangent_in, spectrum, twiddle, mixing, value_taps_in, gate_taps_in, skip_in, cas_in,
    mixed_out, grad_values, grad_gates_out, grad_spectrum_out, value_sums, gate_sums, skip_sums,
    gates, cotangent, cas, params, turned_params, filters_landed, unpacked, spectrum_landed, sums, turned_spectrum,
    fields, filters, factors, short_values, grad_long, wide, weighted,
    spectra, filtered, gradient, out_fields, out_spectrum, totals,
    mixed, grad_gates, grad_spectrum, short_gates, long_here, inner_here, gates_gradient, before, after, rims, line, parts, batch_parts,
    in_send, in_recv, out_send, out_recv, side_send, side_recv, rim_send, rim_recv,
    part_send, part_recv, local,
):
    b, s = lax.axis_index("batch"), lax.axis_index("seq")
    count = batch * seq
    me = b * seq + s
    share, length = fields.shape[2], fields.shape[3]
    block = cas.shape[0]
    blocks = short_values.shape[0] // share
    per_block = block // length
    freqs = block // batch

    def rows_of(bt, st):
        return pl.ds(pl.multiple_of((st * batch + bt) * share, share), share)

    def batch_rows(bt):
        return pl.ds(pl.multiple_of(bt * share, share), share)

    def other(step):
        peer = lax.rem(me + step, count)
        return peer, lax.div(peer, seq), lax.rem(peer, seq)

    def each_other(body):
        @pl.loop(1, count)
        def _(step):
            body(*other(step))

    def each_batch(body):
        for step in range(1, batch):
            body(lax.rem(b + step, batch))

    load_gates = pltpu.make_async_copy(gates_in, gates, local.at[0])
    load_cotangent = pltpu.make_async_copy(cotangent_in, cotangent, local.at[1])
    load_cas = pltpu.make_async_copy(cas_in, cas, local.at[2])
    load_values = pltpu.make_async_copy(values.at[rows_of(b, s), :], fields.at[0, me], local.at[3])
    load_filters = pltpu.make_async_copy(
        spectrum.at[batch_rows(b)], filters_landed.at[b], local.at[4]
    )

    store_values = pltpu.make_async_copy(
        out_fields.at[1, me], grad_values.at[rows_of(b, s), :], local.at[5]
    )
    store_mixed = pltpu.make_async_copy(mixed, mixed_out, local.at[6])
    store_gates = pltpu.make_async_copy(grad_gates, grad_gates_out, local.at[7])
    store_spectrum = pltpu.make_async_copy(grad_spectrum, grad_spectrum_out, local.at[8])

    barrier = pltpu.get_barrier_semaphore()
    each_other(lambda peer, bt, st: pl.semaphore_signal(
        barrier, inc=1, device_id=(bt, st), device_id_type=MESH))
    load_gates.start()
    load_cotangent.start()
    load_values.start()
    load_cas.start()
    load_filters.start()
    turned_params[...] = jnp.zeros_like(turned_params)
    turned_params[0:3, :] = value_taps_in[...]
    turned_params[3:6, :] = gate_taps_in[...]
    turned_params[6:7, :] = skip_in[...]
    params[...] = turned_params[...].T
    load_gates.wait()
    rims[0] = gates[:, length - LANES :].astype(jnp.float32).T[LANES - 8 :, :]
    pl.semaphore_wait(barrier, count - 1)

    def in_copy(n, peer, bt, st):
        return pltpu.make_async_remote_copy(
            src_ref=(values, long_here)[n].at[rows_of(bt, st), :],
            dst_ref=fields.at[n, me],
            send_sem=in_send.at[n],
            recv_sem=in_recv.at[n],
            device_id=(bt, st),
            device_id_type=MESH,
        )

    def out_copy(n, peer, bt, st):
        return pltpu.make_async_remote_copy(
            src_ref=out_fields.at[n, peer],
            dst_ref=(inner_here, grad_values)[n].at[rows_of(b, s), :],
            send_sem=out_send.at[n],
            recv_sem=out_recv.at[n],
            device_id=(bt, st),
            device_id_type=MESH,
        )

    def side_copy(n, bt, slot):
        source = (
            spectrum.at[batch_rows(bt)], twiddle, out_spectrum.at[bt], sums.at[b], batch_parts.at[b]
        )[n]
        target = (
            filters_landed.at[b], factors.at[b], spectrum_landed.at[:, batch_rows(b), :], sums.at[b], batch_parts.at[b]
        )[n]
        return pltpu.make_async_remote_copy(
            src_ref=source,
            dst_ref=target,
            send_sem=side_send.at[n, bt],
            recv_sem=side_recv.at[n, slot],
            device_id=(bt, s),
            device_id_type=MESH,
        )

    def rim_copy(n):
        peer = lax.rem(me + (1, count - 1)[n], count)
        return pltpu.make_async_remote_copy(
            src_ref=rims.at[n],
            dst_ref=rims.at[2 + n],
            send_sem=rim_send.at[n],
            recv_sem=rim_recv.at[n],
            device_id=(lax.div(peer, seq), lax.rem(peer, seq)),
            device_id_type=MESH,
        )

    width = values.shape[0] // seq

    def part_copy(st, slot):
        return pltpu.make_async_remote_copy(
            src_ref=parts.at[0, st],
            dst_ref=parts.at[1, s],
            send_sem=part_send.at[st],
            recv_sem=part_recv.at[slot],
            device_id=(b, st),
            device_id_type=MESH,
        )

    def each_seq(body):
        for step in range(1, seq):
            body(lax.rem(s + step, seq))

    def start_in(n):
        each_other(lambda peer, bt, st: in_copy(n, peer, bt, st).start())

    def wait_all(buffer, semaphore):
        pieces = buffer.at[pl.ds(0, count - 1)]
        pltpu.make_async_copy(pieces, pieces, semaphore).wait()

    def wait_in(n):
        wait_all(fields.at[n], in_recv.at[n])

    def start_out(n):
        each_other(lambda peer, bt, st: out_copy(n, peer, bt, st).start())

    rim_copy(0).start()
    start_in(0)
    each_batch(lambda bt: side_copy(1, bt, b).start())
    each_batch(lambda bt: side_copy(0, bt, b).start())
    factors[b] = twiddle[...]
    totals[...] = jnp.zeros_like(totals)

    lane = lax.broadcasted_iota(jnp.int32, (share, length), 1)
    mine_rows = rows_of(b, s)
    value_taps = [params[mine_rows, n : n + 1] for n in range(3)]
    skip = params[mine_rows, 6:7]
    matrix = [[mixing[p, i] for i in range(blocks)] for p in range(blocks)]

    def delayed_by(now, earlier):
        return [now] + [
            jnp.where(lane < k, pltpu.roll(earlier, k, 1), pltpu.roll(now, k, 1)) for k in (1, 2)
        ]

    def advanced_by(now, later):
        return [now] + [
            jnp.where(
                lane >= length - k, pltpu.roll(later, length - k, 1), pltpu.roll(now, length - k, 1)
            )
            for k in (1, 2)
        ]

    def delays(d):
        now = fields[0, d].astype(jnp.float32)
        earlier = fields[0, jnp.maximum(d - 1, 0)].astype(jnp.float32)
        return delayed_by(now, jnp.where(d > 0, earlier, 0.0))

    def advances(d):
        later = jnp.where(d < count - 1, gradient[jnp.minimum(d + 1, count - 1)], 0.0)
        return advanced_by(gradient[d], later)

    def gate_taps(rows):
        return [params[rows, n : n + 1] for n in range(3, 6)]

    def each_group(body):
        @pl.loop(0, count)
        def _(g):
            body(pl.ds(pl.multiple_of(g * share, share), share))

    def conv(taps, shifted):
        return taps[0] * shifted[0] + taps[1] * shifted[1] + taps[2] * shifted[2]

    def each_chunk(body):
        @pl.loop(0, blocks)
        def _(i):
            for q in range(per_block):
                rows = pl.ds(pl.multiple_of(i * share, share), share)
                body(i * per_block + q, rows, slice(q * length, (q + 1) * length))

    def times_table(source, target):
        tile = min(256, block)

        @pl.loop(0, block // tile)
        def _(at):
            columns = pl.ds(pl.multiple_of(at * tile, tile), tile)
            product = jnp.dot(source[...], cas[:, columns], preferred_element_type=jnp.float32)
            target[:, columns] = product.astype(target.dtype)

    def mix(of_values):
        group = 16

        @pl.loop(0, batch)
        def _(kt):
            for inside in range(0, freqs, LANES):
                columns = pl.ds(pl.multiple_of(kt * freqs + inside, LANES), LANES)
                part = slice(inside, inside + LANES)
                per_batch = blocks // batch
                factor = [
                    factors[i // per_batch, i % per_batch : i % per_batch + 1, columns]
                    for i in range(blocks)
                ]
                for first in range(0, share, group):
                    rows = slice(first, first + group)
                    sums_in = [
                        wide[i * share + first : i * share + first + group, columns] * factor[i]
                        for i in range(blocks)
                    ]
                    products = []
                    for p in range(blocks):
                        mine = matrix[p][0] * sums_in[0]
                        for i in range(1, blocks):
                            mine = mine + matrix[p][i] * sums_in[i]
                        at = slice(p * share + first, p * share + first + group)
                        if of_values:
                            spectra[at, columns] = mine
                        else:
                            out_spectrum[kt, p, rows, part] = (
                                spectra[at, columns] * mine
                            ).astype(out_spectrum.dtype)
                        products.append(mine * filters[kt, p, rows, part])
                    for i in range(blocks):
                        mine = matrix[0][i] * products[0]
                        for p in range(1, blocks):
                            mine = mine + matrix[p][i] * products[p]
                        weighted[i * share + first : i * share + first + group, columns] = (
                            mine * factor[i]
                        ).astype(weighted.dtype)

    load_cotangent.wait()
    rim_copy(0).wait_recv()
    came = jnp.where(me > 0, rims[2], 0.0)
    padded = jnp.concatenate([jnp.zeros((LANES - 8, came.shape[1]), jnp.float32), came], axis=0)
    before[...] = jnp.zeros_like(before)
    before[:, length - LANES :] = padded.T

    @each_group
    def _(rows):
        shifted = delayed_by(gates[rows, :].astype(jnp.float32), before[rows, :])
        short = conv(gate_taps(rows), shifted)
        short_gates[rows, :] = short
        long_here[rows, :] = (cotangent[rows, :].astype(jnp.float32) * short).astype(long_here.dtype)

    start_in(1)
    fields[1, me] = long_here[rows_of(b, s), :]

    load_filters.wait()
    each_batch(lambda bt: side_copy(1, bt, bt).wait_recv())
    each_batch(lambda bt: side_copy(0, bt, bt).wait_recv())
    for bt in range(batch):
        flat = filters_landed[bt].astype(jnp.float32).reshape(share * blocks, freqs)
        for half in range(freqs // LANES):
            lanes = slice(half * LANES, (half + 1) * LANES)
            unpacked[half] = flat[:, lanes]
            for p in range(blocks):
                filters[bt, p, :, lanes] = unpacked[half, pl.ds(p, share, stride=blocks), :]

    load_values.wait()
    wait_in(0)

    @each_chunk
    def _(d, rows, columns):
        short_values[rows, columns] = conv(value_taps, delays(d)).astype(short_values.dtype)

    load_cas.wait()
    times_table(short_values, wide)
    mix(True)
    times_table(weighted, filtered)

    @each_chunk
    def _(d, rows, columns):
        short = short_values[rows, columns].astype(jnp.float32)
        inner = filtered[rows, columns].astype(jnp.float32) + skip * short
        out_fields[0, d] = inner.astype(out_fields.dtype)

    start_out(0)
    inner_here[rows_of(b, s), :] = out_fields[0, me]

    wait_in(1)

    @each_chunk
    def _(d, rows, columns):
        grad_long[rows, columns] = fields[1, d]

    times_table(grad_long, wide)
    mix(False)
    each_batch(lambda bt: side_copy(2, bt, b).start())
    spectrum_landed[:, batch_rows(b), :] = out_spectrum[b]
    times_table(weighted, filtered)

    @each_chunk
    def _(d, rows, columns):
        grads = skip * grad_long[rows, columns].astype(jnp.float32)
        gradient[d] = grads + filtered[rows, columns].astype(jnp.float32)

    @each_chunk
    def _(d, rows, columns):
        out_fields[1, d] = conv(value_taps, advances(d)).astype(out_fields.dtype)

    start_out(1)
    store_values.start()

    column = lax.broadcasted_iota(jnp.int32, (share, LANES), 1)

    def in_columns(columns):
        result = jnp.zeros((share, LANES), jnp.float32)
        for k, value in enumerate(columns):
            result = jnp.where(column == k, jnp.sum(value, axis=1, keepdims=True), result)
        return result

    wait_all(out_fields.at[0], out_recv.at[0])

    @each_group
    def _(rows):
        inner = inner_here[rows, :].astype(jnp.float32)
        mixed[rows, :] = (short_gates[rows, :] * inner).astype(mixed.dtype)
        grads = cotangent[rows, :].astype(jnp.float32) * inner
        gates_gradient[rows, :] = grads
        shifted = delayed_by(gates[rows, :].astype(jnp.float32), before[rows, :])
        line[rows, :] = in_columns([grads * shifted[k] for k in range(3)])

    store_mixed.start()
    rims[1] = gates_gradient[:, :LANES].T[:8, :]
    rim_copy(1).start()
    turned = line[...].T[:8, :]
    for st in range(seq):
        parts[0, st] = turned[:, st * width : (st + 1) * width]
    each_seq(lambda st: part_copy(st, s).start())
    parts[1, s] = parts[0, s]
    @each_chunk
    def _(d, rows, columns):
        shifted = delays(d)
        grads = gradient[d]
        for k in range(3):
            totals[k] += grads * shifted[k]
        totals[3] += grad_long[rows, columns].astype(jnp.float32) * short_values[
            rows, columns
        ].astype(jnp.float32)

    own = in_columns([totals[k] for k in range(4)])
    own = jnp.concatenate([own, jnp.zeros((LANES - share, LANES), jnp.float32)], axis=0)
    sums[b] = own.T[:8, :]
    each_batch(lambda bt: side_copy(3, bt, b).start())

    rim_copy(1).wait_recv()
    came = jnp.where(me < count - 1, rims[3], 0.0)
    padded = jnp.concatenate([came, jnp.zeros((LANES - 8, came.shape[1]), jnp.float32)], axis=0)
    after[...] = jnp.zeros_like(after)
    after[:, :LANES] = padded.T

    @each_group
    def _(rows):
        shifted = advanced_by(gates_gradient[rows, :], after[rows, :])
        grad_gates[rows, :] = conv(gate_taps(rows), shifted).astype(grad_gates.dtype)

    store_gates.start()
    each_batch(lambda bt: side_copy(2, bt, bt).wait_recv())
    for p in range(blocks):
        for half in range(freqs // LANES):
            lanes = slice(half * LANES, (half + 1) * LANES)
            turned_spectrum[half, pl.ds(p, width, stride=blocks), :] = spectrum_landed[p, :, lanes].astype(jnp.float32)
    for half in range(freqs // LANES):
        grad_spectrum[:, half * LANES : (half + 1) * LANES] = turned_spectrum[half]
    store_spectrum.start()
    each_seq(lambda st: part_copy(st, st).wait_recv())
    total = parts[1, 0]
    for st in range(1, seq):
        total = total + parts[1, st]
    batch_parts[b] = total
    each_batch(lambda bt: side_copy(4, bt, b).start())
    each_batch(lambda bt: side_copy(4, bt, bt).wait_recv())
    total = batch_parts[0]
    for bt in range(1, batch):
        total = total + batch_parts[bt]
    gate_sums[...] = total[:3, :]

    each_batch(lambda bt: side_copy(3, bt, bt).wait_recv())
    total = jnp.concatenate([sums[bt, :, :share] for bt in range(batch)], axis=1)
    value_sums[...] = total[:3, :]
    skip_sums[...] = total[3:4, :]

    each_seq(lambda st: part_copy(st, s).wait_send())
    for n in range(2):
        rim_copy(n).wait_send()
        wait_all(fields.at[n], in_send.at[n])
        wait_all(out_fields.at[n], out_send.at[n])
    for n in range(5):
        each_batch(lambda bt: side_copy(n, bt, b).wait_send())
    for store in (store_values, store_mixed, store_gates, store_spectrum):
        store.wait()
    wait_all(out_fields.at[1], out_recv.at[1])


def hand_over(*refs):
    count = len(refs) // 2
    sources, targets, semaphores = refs[:count], refs[count : 2 * count], refs[-1]
    copies = []
    for n, (source, target) in enumerate(zip(sources, targets)):
        parts = 4 if source.shape[0] % 64 == 0 else 1
        rows = source.shape[0] // parts
        for part in range(parts):
            at = pl.ds(part * rows, rows)
            copies.append(
                pltpu.make_async_copy(source.at[at], target.at[at], semaphores.at[n, part])
            )
    for copy in copies:
        copy.start()
    for copy in copies:
        copy.wait()


def per_device_kernel(
    values, gates, cotangent, taps_values, taps_gates, skip_gain, twiddle, mixing, spectrum
):
    batch, seq = lax.axis_size("batch"), lax.axis_size("seq")
    count = batch * seq
    channels, length = values.shape
    share = channels // count
    blocks, block = mixing.shape[0], twiddle.shape[1]
    freqs = block // batch
    vmem = pl.BlockSpec(memory_space=pltpu.VMEM)
    hbm = pl.BlockSpec(memory_space=pl.ANY)
    smem = pl.BlockSpec(memory_space=pltpu.SMEM)
    field = jax.ShapeDtypeStruct((channels, length), jnp.bfloat16)
    rows = blocks * share
    results = pl.pallas_call(
        functools.partial(whole_sequences, batch, seq),
        out_shape=[
            field, field, field,
            jax.ShapeDtypeStruct((blocks * channels // seq, freqs), jnp.float32),
            jax.ShapeDtypeStruct((3, channels // seq), jnp.float32),
            jax.ShapeDtypeStruct((3, channels // seq), jnp.float32),
            jax.ShapeDtypeStruct((1, channels // seq), jnp.float32),
        ],
        in_specs=[hbm, hbm, hbm, hbm, vmem, smem, vmem, vmem, vmem, hbm],
        out_specs=[hbm] * 4 + [vmem] * 3,
        scratch_shapes=[
            pltpu.VMEM((channels, length), jnp.bfloat16),
            pltpu.VMEM((channels, length), jnp.bfloat16),
            pltpu.VMEM((block, block), jnp.bfloat16),
            pltpu.VMEM((channels, LANES), jnp.float32),
            pltpu.VMEM((LANES, channels), jnp.float32),
            pltpu.VMEM((batch, share, blocks, freqs), jnp.bfloat16),
            pltpu.VMEM((freqs // LANES, share * blocks, LANES), jnp.float32),
            pltpu.VMEM((blocks, channels // seq, freqs), jnp.bfloat16),
            pltpu.VMEM((batch, 8, LANES), jnp.float32),
            pltpu.VMEM((freqs // LANES, blocks * channels // seq, LANES), jnp.float32),
            pltpu.VMEM((2, count, share, length), jnp.bfloat16),
            pltpu.VMEM((batch, blocks, share, freqs), jnp.float32),
            pltpu.VMEM((batch, blocks // batch, block), jnp.float32),
            pltpu.VMEM((rows, block), jnp.bfloat16),
            pltpu.VMEM((rows, block), jnp.bfloat16),
            pltpu.VMEM((rows, block), jnp.float32),
            pltpu.VMEM((rows, block), jnp.bfloat16),
            pltpu.VMEM((rows, block), jnp.float32),
            pltpu.VMEM((rows, block), jnp.bfloat16),
            pltpu.VMEM((count, share, length), jnp.float32),
            pltpu.VMEM((2, count, share, length), jnp.bfloat16),
            pltpu.VMEM((batch, blocks, share, freqs), jnp.bfloat16),
            pltpu.VMEM((4, share, length), jnp.float32),
            pltpu.VMEM((channels, length), jnp.bfloat16),
            pltpu.VMEM((channels, length), jnp.bfloat16),
            pltpu.VMEM((blocks * channels // seq, freqs), jnp.float32),
            pltpu.VMEM((channels, length), jnp.float32),
            pltpu.VMEM((channels, length), jnp.bfloat16),
            pltpu.VMEM((channels, length), jnp.bfloat16),
            pltpu.VMEM((channels, length), jnp.float32),
            pltpu.VMEM((channels, length), jnp.float32),
            pltpu.VMEM((channels, length), jnp.float32),
            pltpu.VMEM((4, 8, channels), jnp.float32),
            pltpu.VMEM((channels, LANES), jnp.float32),
            pltpu.VMEM((2, seq, 8, channels // seq), jnp.float32),
            pltpu.VMEM((batch, 8, channels // seq), jnp.float32),
            pltpu.SemaphoreType.DMA((2,)),
            pltpu.SemaphoreType.DMA((2,)),
            pltpu.SemaphoreType.DMA((2,)),
            pltpu.SemaphoreType.DMA((2,)),
            pltpu.SemaphoreType.DMA((5, batch)),
            pltpu.SemaphoreType.DMA((5, batch)),
            pltpu.SemaphoreType.DMA((2,)),
            pltpu.SemaphoreType.DMA((2,)),
            pltpu.SemaphoreType.DMA((seq,)),
            pltpu.SemaphoreType.DMA((seq,)),
            pltpu.SemaphoreType.DMA((9,)),
        ],
        compiler_params=pltpu.CompilerParams(
            collective_id=0, has_side_effects=True, vmem_limit_bytes=56 * 2**20
        ),
    )(
        values, gates, cotangent, spectrum, twiddle, mixing, taps_values, taps_gates,
        skip_gain[None], cas_table(block),
    )
    mixed, grad_values, grad_gates, grad_spectrum, value_sums, gate_sums, skip_sums = pl.pallas_call(
        hand_over,
        out_shape=[jax.ShapeDtypeStruct(one.shape, one.dtype) for one in results],
        in_specs=[hbm] * len(results),
        out_specs=[hbm] * len(results),
        scratch_shapes=[pltpu.SemaphoreType.DMA((len(results), 4))],
        compiler_params=pltpu.CompilerParams(vmem_limit_bytes=56 * 2**20),
    )(*results)
    grad_spectrum = grad_spectrum.reshape(channels // seq, blocks, freqs)
    return (
        mixed, grad_values, grad_gates, grad_spectrum, value_sums, gate_sums, skip_sums[0]
    )


def per_device(values, *rest):
    twiddle, mixing = rest[5], rest[6]
    batch = lax.axis_size("batch")
    count = batch * lax.axis_size("seq")
    channels, length = values.shape
    block = twiddle.shape[1]
    fits = (
        channels % (count * 16) == 0
        and length % LANES == 0
        and channels % (lax.axis_size("seq") * LANES) == 0
        and block % length == 0
        and block % (batch * LANES) == 0
        and mixing.shape[0] % batch == 0
        and mixing.shape[0] % 8 == 0
        and channels // count <= LANES
    )
    return (per_device_kernel if fits else per_device_plain)(values, *rest)


def solution(mesh):
    spread = P(None, AXES)
    in_specs = (
        spread, spread, spread, P(), P(), P(), P("batch", None), P(), P("seq", None, "batch")
    )
    out_specs = (
        spread, spread, spread, P("seq", None, "batch"), P(None, "seq"), P(None, "seq"), P("seq")
    )
    return jax.shard_map(
        per_device, mesh=mesh, in_specs=in_specs, out_specs=out_specs, check_vma=False
    )
```

```python
import functools
import math

import jax
import jax.numpy as jnp
import numpy as np
from jax import lax
from jax.experimental import pallas as pl
from jax.experimental.pallas import tpu as pltpu
from jax.sharding import PartitionSpec as P

AXES = ("batch", "seq")


def cas_table(block):
    angles = np.arange(block, dtype=np.float32) * np.float32(2.0 * math.pi / block)
    entries = (np.cos(angles) + np.sin(angles)) / np.float32(math.sqrt(block))
    indices = np.arange(block)
    return jnp.asarray(entries.astype(jnp.bfloat16)[indices[:, None] * indices[None, :] % block])


def delayed(field, steps):
    return jnp.pad(field, ((0, 0), (steps, 0)))[:, : field.shape[1]]


def advanced(field, steps):
    return jnp.pad(field, ((0, 0), (0, steps)))[:, steps:]


def short_conv(field, taps, shift):
    return (
        taps[0][:, None] * field
        + taps[1][:, None] * shift(field, 1)
        + taps[2][:, None] * shift(field, 2)
    )


def tap_sums(gradient, field):
    return jnp.stack([jnp.sum(gradient * delayed(field, s), axis=1) for s in range(3)])


def per_device_plain(
    values, gates, cotangent, taps_values, taps_gates, skip_gain, twiddle, mixing, spectrum
):
    block = twiddle.shape[1]
    cas = cas_table(block)
    batch, seq = lax.axis_size("batch"), lax.axis_size("seq")
    share = values.shape[0] // (batch * seq)
    b, s = lax.axis_index("batch"), lax.axis_index("seq")
    start = (s * batch + b) * share
    stacked = jnp.stack([values, gates, cotangent])
    length_dev = values.shape[1]
    stacked = stacked.reshape(3, seq, batch, share, length_dev).transpose(2, 1, 0, 3, 4)
    stacked = stacked.reshape(batch * seq, 3, share, length_dev)
    whole = lax.all_to_all(stacked, AXES, split_axis=0, concat_axis=0, tiled=True)
    whole = whole.transpose(1, 2, 0, 3).reshape(3, share, -1)
    filters = lax.all_to_all(spectrum, "batch", split_axis=0, concat_axis=2, tiled=True)
    filters = filters.astype(jnp.float32)
    factors = lax.all_gather(twiddle, "batch", axis=0, tiled=True)
    params = jnp.concatenate([taps_values, taps_gates, skip_gain[None]], axis=0)
    params = lax.dynamic_slice_in_dim(params, start, share, 1)
    value_taps, gate_taps, skip = params[:3], params[3:6], params[6][:, None]
    field, gate, cot = (whole[n].astype(jnp.float32) for n in range(3))
    short_values = short_conv(field, value_taps, delayed).astype(jnp.bfloat16)
    short_gates = short_conv(gate, gate_taps, delayed)
    grad_long = (cot * short_gates).astype(jnp.bfloat16)

    def transform(source):
        sums = jnp.dot(source.reshape(-1, block), cas, preferred_element_type=jnp.float32)
        sums = sums.reshape(share, -1, block) * factors
        return jnp.einsum("pi,cik->cpk", mixing, sums, precision=lax.Precision.HIGHEST)

    def back(spectra):
        mixed = jnp.einsum("pi,cpk->cik", mixing, spectra, precision=lax.Precision.HIGHEST)
        weighted = (mixed * factors).astype(jnp.bfloat16)
        result = jnp.dot(weighted.reshape(-1, block), cas, preferred_element_type=jnp.float32)
        return result.reshape(share, -1).astype(jnp.bfloat16).astype(jnp.float32)

    spectra_values, spectra_grads = transform(short_values), transform(grad_long)
    long_values, back_grads = back(spectra_values * filters), back(spectra_grads * filters)
    grad_spectrum = (spectra_values * spectra_grads).astype(jnp.bfloat16)
    grad_spectrum = lax.all_to_all(grad_spectrum, "batch", split_axis=2, concat_axis=0, tiled=True)
    short_f32 = short_values.astype(jnp.float32)
    long_f32 = grad_long.astype(jnp.float32)
    inner = long_values + skip * short_f32
    grad_short_gates = cot * inner
    grad_short_values = skip * long_f32 + back_grads
    outs = jnp.stack([
        (short_gates * inner).astype(jnp.bfloat16),
        short_conv(grad_short_values, value_taps, advanced).astype(jnp.bfloat16),
        short_conv(grad_short_gates, gate_taps, advanced).astype(jnp.bfloat16),
    ])
    outs = outs.reshape(3, share, batch * seq, length_dev).transpose(2, 0, 1, 3)
    outs = lax.all_to_all(outs, AXES, split_axis=0, concat_axis=0, tiled=True)
    outs = outs.reshape(batch, seq, 3, share, length_dev).transpose(2, 1, 0, 3, 4)
    outs = outs.reshape(3, -1, length_dev)
    sums = jnp.concatenate([
        tap_sums(grad_short_values, field),
        tap_sums(grad_short_gates, gate),
        jnp.sum(long_f32 * short_f32, axis=1)[None],
    ])
    sums = lax.all_gather(sums, "batch", axis=1, tiled=True)
    return (
        outs[0], outs[1], outs[2], grad_spectrum.astype(jnp.float32), sums[:3], sums[3:6], sums[6]
    )


LANES = 128
MESH = pl.DeviceIdType.MESH


def whole_sequences(
    batch, seq,
    values, gates_in, cotangent_in, spectrum, twiddle, mixing, value_taps_in, gate_taps_in, skip_in, cas_in,
    mixed_out, grad_values, grad_gates_out, grad_spectrum_out, value_sums, gate_sums, skip_sums,
    gates, cotangent, cas, params, turned_params, filters_landed, unpacked, spectrum_landed, sums, turned_spectrum,
    fields, filters, factors, short_values, grad_long, wide, weighted,
    spectra, filtered, gradient, out_fields, out_spectrum, totals,
    mixed, grad_gates, grad_spectrum, short_gates, long_here, inner_here, gates_gradient, before, after, rims, line, parts, batch_parts,
    in_send, in_recv, out_send, out_recv, side_send, side_recv, rim_send, rim_recv,
    part_send, part_recv, local,
):
    b, s = lax.axis_index("batch"), lax.axis_index("seq")
    count = batch * seq
    me = b * seq + s
    share, length = fields.shape[2], fields.shape[3]
    block = cas.shape[0]
    blocks = short_values.shape[0] // share
    per_block = block // length
    freqs = block // batch

    def rows_of(bt, st):
        return pl.ds(pl.multiple_of((st * batch + bt) * share, share), share)

    def batch_rows(bt):
        return pl.ds(pl.multiple_of(bt * share, share), share)

    def other(step):
        peer = lax.rem(me + step, count)
        return peer, lax.div(peer, seq), lax.rem(peer, seq)

    def each_other(body):
        @pl.loop(1, count)
        def _(step):
            body(*other(step))

    def each_batch(body):
        for step in range(1, batch):
            body(lax.rem(b + step, batch))

    load_gates = pltpu.make_async_copy(gates_in, gates, local.at[0])
    load_cotangent = pltpu.make_async_copy(cotangent_in, cotangent, local.at[1])
    load_cas = pltpu.make_async_copy(cas_in, cas, local.at[2])
    load_values = pltpu.make_async_copy(values.at[rows_of(b, s), :], fields.at[0, me], local.at[3])
    load_filters = pltpu.make_async_copy(
        spectrum.at[batch_rows(b)], filters_landed.at[b], local.at[4]
    )

    store_values = pltpu.make_async_copy(
        out_fields.at[1, me], grad_values.at[rows_of(b, s), :], local.at[5]
    )
    store_mixed = pltpu.make_async_copy(mixed, mixed_out, local.at[6])
    store_gates = pltpu.make_async_copy(grad_gates, grad_gates_out, local.at[7])
    store_spectrum = pltpu.make_async_copy(grad_spectrum, grad_spectrum_out, local.at[8])

    barrier = pltpu.get_barrier_semaphore()
    each_other(lambda peer, bt, st: pl.semaphore_signal(
        barrier, inc=1, device_id=(bt, st), device_id_type=MESH))
    load_gates.start()
    load_cotangent.start()
    load_values.start()
    load_cas.start()
    load_filters.start()
    turned_params[...] = jnp.zeros_like(turned_params)
    turned_params[0:3, :] = value_taps_in[...]
    turned_params[3:6, :] = gate_taps_in[...]
    turned_params[6:7, :] = skip_in[...]
    params[...] = turned_params[...].T
    load_gates.wait()
    rims[0] = gates[:, length - LANES :].astype(jnp.float32).T[LANES - 8 :, :]
    pl.semaphore_wait(barrier, count - 1)

    def in_copy(n, peer, bt, st):
        return pltpu.make_async_remote_copy(
            src_ref=(values, long_here)[n].at[rows_of(bt, st), :],
            dst_ref=fields.at[n, me],
            send_sem=in_send.at[n],
            recv_sem=in_recv.at[n],
            device_id=(bt, st),
            device_id_type=MESH,
        )

    def out_copy(n, peer, bt, st):
        return pltpu.make_async_remote_copy(
            src_ref=out_fields.at[n, peer],
            dst_ref=(inner_here, grad_values)[n].at[rows_of(b, s), :],
            send_sem=out_send.at[n],
            recv_sem=out_recv.at[n],
            device_id=(bt, st),
            device_id_type=MESH,
        )

    def side_copy(n, bt, slot):
        source = (
            spectrum.at[batch_rows(bt)], twiddle, out_spectrum.at[bt], sums.at[b], batch_parts.at[b]
        )[n]
        target = (
            filters_landed.at[b], factors.at[b], spectrum_landed.at[:, batch_rows(b), :], sums.at[b], batch_parts.at[b]
        )[n]
        return pltpu.make_async_remote_copy(
            src_ref=source,
            dst_ref=target,
            send_sem=side_send.at[n, bt],
            recv_sem=side_recv.at[n, slot],
            device_id=(bt, s),
            device_id_type=MESH,
        )

    def rim_copy(n):
        peer = lax.rem(me + (1, count - 1)[n], count)
        return pltpu.make_async_remote_copy(
            src_ref=rims.at[n],
            dst_ref=rims.at[2 + n],
            send_sem=rim_send.at[n],
            recv_sem=rim_recv.at[n],
            device_id=(lax.div(peer, seq), lax.rem(peer, seq)),
            device_id_type=MESH,
        )

    width = values.shape[0] // seq

    def part_copy(st, slot):
        return pltpu.make_async_remote_copy(
            src_ref=parts.at[0, st],
            dst_ref=parts.at[1, s],
            send_sem=part_send.at[st],
            recv_sem=part_recv.at[slot],
            device_id=(b, st),
            device_id_type=MESH,
        )

    def each_seq(body):
        for step in range(1, seq):
            body(lax.rem(s + step, seq))

    def start_in(n):
        each_other(lambda peer, bt, st: in_copy(n, peer, bt, st).start())

    def wait_all(buffer, semaphore):
        pieces = buffer.at[pl.ds(0, count - 1)]
        pltpu.make_async_copy(pieces, pieces, semaphore).wait()

    def wait_in(n):
        wait_all(fields.at[n], in_recv.at[n])

    def start_out(n):
        each_other(lambda peer, bt, st: out_copy(n, peer, bt, st).start())

    rim_copy(0).start()
    start_in(0)
    each_batch(lambda bt: side_copy(1, bt, b).start())
    each_batch(lambda bt: side_copy(0, bt, b).start())
    factors[b] = twiddle[...]
    totals[...] = jnp.zeros_like(totals)

    lane = lax.broadcasted_iota(jnp.int32, (share, length), 1)
    mine_rows = rows_of(b, s)
    value_taps = [params[mine_rows, n : n + 1] for n in range(3)]
    skip = params[mine_rows, 6:7]
    matrix = [[mixing[p, i] for i in range(blocks)] for p in range(blocks)]

    def delayed_by(now, earlier):
        return [now] + [
            jnp.where(lane < k, pltpu.roll(earlier, k, 1), pltpu.roll(now, k, 1)) for k in (1, 2)
        ]

    def advanced_by(now, later):
        return [now] + [
            jnp.where(
                lane >= length - k, pltpu.roll(later, length - k, 1), pltpu.roll(now, length - k, 1)
            )
            for k in (1, 2)
        ]

    def delays(d):
        now = fields[0, d].astype(jnp.float32)
        earlier = fields[0, jnp.maximum(d - 1, 0)].astype(jnp.float32)
        return delayed_by(now, jnp.where(d > 0, earlier, 0.0))

    def advances(d):
        later = jnp.where(d < count - 1, gradient[jnp.minimum(d + 1, count - 1)], 0.0)
        return advanced_by(gradient[d], later)

    def gate_taps(rows):
        return [params[rows, n : n + 1] for n in range(3, 6)]

    def each_group(body):
        @pl.loop(0, count)
        def _(g):
            body(pl.ds(pl.multiple_of(g * share, share), share))

    def conv(taps, shifted):
        return taps[0] * shifted[0] + taps[1] * shifted[1] + taps[2] * shifted[2]

    def each_chunk(body):
        @pl.loop(0, blocks)
        def _(i):
            for q in range(per_block):
                rows = pl.ds(pl.multiple_of(i * share, share), share)
                body(i * per_block + q, rows, slice(q * length, (q + 1) * length))

    def times_table(source, target):
        tile = min(256, block)

        @pl.loop(0, block // tile)
        def _(at):
            columns = pl.ds(pl.multiple_of(at * tile, tile), tile)
            product = jnp.dot(source[...], cas[:, columns], preferred_element_type=jnp.float32)
            target[:, columns] = product.astype(target.dtype)

    def mix(of_values):
        group = 16

        @pl.loop(0, batch)
        def _(kt):
            for inside in range(0, freqs, LANES):
                columns = pl.ds(pl.multiple_of(kt * freqs + inside, LANES), LANES)
                part = slice(inside, inside + LANES)
                per_batch = blocks // batch
                factor = [
                    factors[i // per_batch, i % per_batch : i % per_batch + 1, columns]
                    for i in range(blocks)
                ]
                for first in range(0, share, group):
                    rows = slice(first, first + group)
                    sums_in = [
                        wide[i * share + first : i * share + first + group, columns] * factor[i]
                        for i in range(blocks)
                    ]
                    products = []
                    for p in range(blocks):
                        mine = matrix[p][0] * sums_in[0]
                        for i in range(1, blocks):
                            mine = mine + matrix[p][i] * sums_in[i]
                        at = slice(p * share + first, p * share + first + group)
                        if of_values:
                            spectra[at, columns] = mine
                        else:
                            out_spectrum[kt, p, rows, part] = (
                                spectra[at, columns] * mine
                            ).astype(out_spectrum.dtype)
                        products.append(mine * filters[kt, p, rows, part])
                    for i in range(blocks):
                        mine = matrix[0][i] * products[0]
                        for p in range(1, blocks):
                            mine = mine + matrix[p][i] * products[p]
                        weighted[i * share + first : i * share + first + group, columns] = (
                            mine * factor[i]
                        ).astype(weighted.dtype)

    load_cotangent.wait()
    rim_copy(0).wait_recv()
    came = jnp.where(me > 0, rims[2], 0.0)
    padded = jnp.concatenate([jnp.zeros((LANES - 8, came.shape[1]), jnp.float32), came], axis=0)
    before[...] = jnp.zeros_like(before)
    before[:, length - LANES :] = padded.T

    @each_group
    def _(rows):
        shifted = delayed_by(gates[rows, :].astype(jnp.float32), before[rows, :])
        short = conv(gate_taps(rows), shifted)
        short_gates[rows, :] = short
        long_here[rows, :] = (cotangent[rows, :].astype(jnp.float32) * short).astype(long_here.dtype)

    start_in(1)
    fields[1, me] = long_here[rows_of(b, s), :]

    load_filters.wait()
    each_batch(lambda bt: side_copy(1, bt, bt).wait_recv())
    each_batch(lambda bt: side_copy(0, bt, bt).wait_recv())
    for bt in range(batch):
        flat = filters_landed[bt].astype(jnp.float32).reshape(share * blocks, freqs)
        for half in range(freqs // LANES):
            lanes = slice(half * LANES, (half + 1) * LANES)
            unpacked[half] = flat[:, lanes]
            for p in range(blocks):
                filters[bt, p, :, lanes] = unpacked[half, pl.ds(p, share, stride=blocks), :]

    load_values.wait()
    wait_in(0)

    @each_chunk
    def _(d, rows, columns):
        short_values[rows, columns] = conv(value_taps, delays(d)).astype(short_values.dtype)

    load_cas.wait()
    times_table(short_values, wide)
    mix(True)
    times_table(weighted, filtered)

    @each_chunk
    def _(d, rows, columns):
        short = short_values[rows, columns].astype(jnp.float32)
        inner = filtered[rows, columns].astype(jnp.float32) + skip * short
        out_fields[0, d] = inner.astype(out_fields.dtype)

    start_out(0)
    inner_here[rows_of(b, s), :] = out_fields[0, me]

    wait_in(1)

    @each_chunk
    def _(d, rows, columns):
        grad_long[rows, columns] = fields[1, d]

    times_table(grad_long, wide)
    mix(False)
    each_batch(lambda bt: side_copy(2, bt, b).start())
    spectrum_landed[:, batch_rows(b), :] = out_spectrum[b]
    times_table(weighted, filtered)

    @each_chunk
    def _(d, rows, columns):
        grads = skip * grad_long[rows, columns].astype(jnp.float32)
        gradient[d] = grads + filtered[rows, columns].astype(jnp.float32)

    @each_chunk
    def _(d, rows, columns):
        out_fields[1, d] = conv(value_taps, advances(d)).astype(out_fields.dtype)

    start_out(1)
    store_values.start()

    column = lax.broadcasted_iota(jnp.int32, (share, LANES), 1)

    def in_columns(columns):
        result = jnp.zeros((share, LANES), jnp.float32)
        for k, value in enumerate(columns):
            result = jnp.where(column == k, jnp.sum(value, axis=1, keepdims=True), result)
        return result

    wait_all(out_fields.at[0], out_recv.at[0])

    @each_group
    def _(rows):
        inner = inner_here[rows, :].astype(jnp.float32)
        mixed[rows, :] = (short_gates[rows, :] * inner).astype(mixed.dtype)
        grads = cotangent[rows, :].astype(jnp.float32) * inner
        gates_gradient[rows, :] = grads
        shifted = delayed_by(gates[rows, :].astype(jnp.float32), before[rows, :])
        line[rows, :] = in_columns([grads * shifted[k] for k in range(3)])

    store_mixed.start()
    rims[1] = gates_gradient[:, :LANES].T[:8, :]
    rim_copy(1).start()
    turned = line[...].T[:8, :]
    for st in range(seq):
        parts[0, st] = turned[:, st * width : (st + 1) * width]
    each_seq(lambda st: part_copy(st, s).start())
    parts[1, s] = parts[0, s]
    @each_chunk
    def _(d, rows, columns):
        shifted = delays(d)
        grads = gradient[d]
        for k in range(3):
            totals[k] += grads * shifted[k]
        totals[3] += grad_long[rows, columns].astype(jnp.float32) * short_values[
            rows, columns
        ].astype(jnp.float32)

    own = in_columns([totals[k] for k in range(4)])
    own = jnp.concatenate([own, jnp.zeros((LANES - share, LANES), jnp.float32)], axis=0)
    sums[b] = own.T[:8, :]
    each_batch(lambda bt: side_copy(3, bt, b).start())

    rim_copy(1).wait_recv()
    came = jnp.where(me < count - 1, rims[3], 0.0)
    padded = jnp.concatenate([came, jnp.zeros((LANES - 8, came.shape[1]), jnp.float32)], axis=0)
    after[...] = jnp.zeros_like(after)
    after[:, :LANES] = padded.T

    @each_group
    def _(rows):
        shifted = advanced_by(gates_gradient[rows, :], after[rows, :])
        grad_gates[rows, :] = conv(gate_taps(rows), shifted).astype(grad_gates.dtype)

    store_gates.start()
    each_batch(lambda bt: side_copy(2, bt, bt).wait_recv())
    for p in range(blocks):
        for half in range(freqs // LANES):
            lanes = slice(half * LANES, (half + 1) * LANES)
            turned_spectrum[half, pl.ds(p, width, stride=blocks), :] = spectrum_landed[p, :, lanes].astype(jnp.float32)
    for half in range(freqs // LANES):
        grad_spectrum[:, half * LANES : (half + 1) * LANES] = turned_spectrum[half]
    store_spectrum.start()
    each_seq(lambda st: part_copy(st, st).wait_recv())
    total = parts[1, 0]
    for st in range(1, seq):
        total = total + parts[1, st]
    batch_parts[b] = total
    each_batch(lambda bt: side_copy(4, bt, b).start())
    each_batch(lambda bt: side_copy(4, bt, bt).wait_recv())
    total = batch_parts[0]
    for bt in range(1, batch):
        total = total + batch_parts[bt]
    gate_sums[...] = total[:3, :]

    each_batch(lambda bt: side_copy(3, bt, bt).wait_recv())
    total = jnp.concatenate([sums[bt, :, :share] for bt in range(batch)], axis=1)
    value_sums[...] = total[:3, :]
    skip_sums[...] = total[3:4, :]

    each_seq(lambda st: part_copy(st, s).wait_send())
    for n in range(2):
        rim_copy(n).wait_send()
        wait_all(fields.at[n], in_send.at[n])
        wait_all(out_fields.at[n], out_send.at[n])
    for n in range(5):
        each_batch(lambda bt: side_copy(n, bt, b).wait_send())
    for store in (store_values, store_mixed, store_gates, store_spectrum):
        store.wait()
    wait_all(out_fields.at[1], out_recv.at[1])


def hand_over(count, *refs):
    sources, targets, held = refs[:count], refs[count : 2 * count], refs[2 * count : 3 * count]
    arrive, leave = refs[3 * count :]
    steps = []
    for n, (source, target) in enumerate(zip(sources, targets)):
        parts = 4 if source.shape[0] % 64 == 0 else 1
        rows = source.shape[0] // parts
        for part in range(parts):
            at = pl.ds(part * rows, rows)
            steps.append((
                pltpu.make_async_copy(source.at[at], held[n].at[at], arrive.at[n, part]),
                pltpu.make_async_copy(held[n].at[at], target.at[at], leave.at[n, part]),
            ))
    for come, _ in steps:
        come.start()
    for come, go in steps:
        come.wait()
        go.start()
    for _, go in steps:
        go.wait()


def per_device_kernel(
    values, gates, cotangent, taps_values, taps_gates, skip_gain, twiddle, mixing, spectrum
):
    batch, seq = lax.axis_size("batch"), lax.axis_size("seq")
    count = batch * seq
    channels, length = values.shape
    share = channels // count
    blocks, block = mixing.shape[0], twiddle.shape[1]
    freqs = block // batch
    vmem = pl.BlockSpec(memory_space=pltpu.VMEM)
    hbm = pl.BlockSpec(memory_space=pl.ANY)
    smem = pl.BlockSpec(memory_space=pltpu.SMEM)
    field = jax.ShapeDtypeStruct((channels, length), jnp.bfloat16)
    rows = blocks * share
    results = pl.pallas_call(
        functools.partial(whole_sequences, batch, seq),
        out_shape=[
            field, field, field,
            jax.ShapeDtypeStruct((blocks * channels // seq, freqs), jnp.float32),
            jax.ShapeDtypeStruct((3, channels // seq), jnp.float32),
            jax.ShapeDtypeStruct((3, channels // seq), jnp.float32),
            jax.ShapeDtypeStruct((1, channels // seq), jnp.float32),
        ],
        in_specs=[hbm, hbm, hbm, hbm, vmem, smem, vmem, vmem, vmem, hbm],
        out_specs=[hbm] * 4 + [vmem] * 3,
        scratch_shapes=[
            pltpu.VMEM((channels, length), jnp.bfloat16),
            pltpu.VMEM((channels, length), jnp.bfloat16),
            pltpu.VMEM((block, block), jnp.bfloat16),
            pltpu.VMEM((channels, LANES), jnp.float32),
            pltpu.VMEM((LANES, channels), jnp.float32),
            pltpu.VMEM((batch, share, blocks, freqs), jnp.bfloat16),
            pltpu.VMEM((freqs // LANES, share * blocks, LANES), jnp.float32),
            pltpu.VMEM((blocks, channels // seq, freqs), jnp.bfloat16),
            pltpu.VMEM((batch, 8, LANES), jnp.float32),
            pltpu.VMEM((freqs // LANES, blocks * channels // seq, LANES), jnp.float32),
            pltpu.VMEM((2, count, share, length), jnp.bfloat16),
            pltpu.VMEM((batch, blocks, share, freqs), jnp.float32),
            pltpu.VMEM((batch, blocks // batch, block), jnp.float32),
            pltpu.VMEM((rows, block), jnp.bfloat16),
            pltpu.VMEM((rows, block), jnp.bfloat16),
            pltpu.VMEM((rows, block), jnp.float32),
            pltpu.VMEM((rows, block), jnp.bfloat16),
            pltpu.VMEM((rows, block), jnp.float32),
            pltpu.VMEM((rows, block), jnp.bfloat16),
            pltpu.VMEM((count, share, length), jnp.float32),
            pltpu.VMEM((2, count, share, length), jnp.bfloat16),
            pltpu.VMEM((batch, blocks, share, freqs), jnp.bfloat16),
            pltpu.VMEM((4, share, length), jnp.float32),
            pltpu.VMEM((channels, length), jnp.bfloat16),
            pltpu.VMEM((channels, length), jnp.bfloat16),
            pltpu.VMEM((blocks * channels // seq, freqs), jnp.float32),
            pltpu.VMEM((channels, length), jnp.float32),
            pltpu.VMEM((channels, length), jnp.bfloat16),
            pltpu.VMEM((channels, length), jnp.bfloat16),
            pltpu.VMEM((channels, length), jnp.float32),
            pltpu.VMEM((channels, length), jnp.float32),
            pltpu.VMEM((channels, length), jnp.float32),
            pltpu.VMEM((4, 8, channels), jnp.float32),
            pltpu.VMEM((channels, LANES), jnp.float32),
            pltpu.VMEM((2, seq, 8, channels // seq), jnp.float32),
            pltpu.VMEM((batch, 8, channels // seq), jnp.float32),
            pltpu.SemaphoreType.DMA((2,)),
            pltpu.SemaphoreType.DMA((2,)),
            pltpu.SemaphoreType.DMA((2,)),
            pltpu.SemaphoreType.DMA((2,)),
            pltpu.SemaphoreType.DMA((5, batch)),
            pltpu.SemaphoreType.DMA((5, batch)),
            pltpu.SemaphoreType.DMA((2,)),
            pltpu.SemaphoreType.DMA((2,)),
            pltpu.SemaphoreType.DMA((seq,)),
            pltpu.SemaphoreType.DMA((seq,)),
            pltpu.SemaphoreType.DMA((9,)),
        ],
        compiler_params=pltpu.CompilerParams(
            collective_id=0, has_side_effects=True, vmem_limit_bytes=56 * 2**20
        ),
    )(
        values, gates, cotangent, spectrum, twiddle, mixing, taps_values, taps_gates,
        skip_gain[None], cas_table(block),
    )
    mixed, grad_values, grad_gates, grad_spectrum, value_sums, gate_sums, skip_sums = pl.pallas_call(
        functools.partial(hand_over, len(results)),
        out_shape=[jax.ShapeDtypeStruct(one.shape, one.dtype) for one in results],
        in_specs=[hbm] * len(results),
        out_specs=[hbm] * len(results),
        scratch_shapes=[pltpu.VMEM(one.shape, one.dtype) for one in results]
        + [pltpu.SemaphoreType.DMA((len(results), 4))] * 2,
        compiler_params=pltpu.CompilerParams(vmem_limit_bytes=56 * 2**20),
    )(*results)
    grad_spectrum = grad_spectrum.reshape(channels // seq, blocks, freqs)
    return (
        mixed, grad_values, grad_gates, grad_spectrum, value_sums, gate_sums, skip_sums[0]
    )


def per_device(values, *rest):
    twiddle, mixing = rest[5], rest[6]
    batch = lax.axis_size("batch")
    count = batch * lax.axis_size("seq")
    channels, length = values.shape
    block = twiddle.shape[1]
    fits = (
        channels % (count * 16) == 0
        and length % LANES == 0
        and channels % (lax.axis_size("seq") * LANES) == 0
        and block % length == 0
        and block % (batch * LANES) == 0
        and mixing.shape[0] % batch == 0
        and mixing.shape[0] % 8 == 0
        and channels // count <= LANES
    )
    return (per_device_kernel if fits else per_device_plain)(values, *rest)


def solution(mesh):
    spread = P(None, AXES)
    in_specs = (
        spread, spread, spread, P(), P(), P(), P("batch", None), P(), P("seq", None, "batch")
    )
    out_specs = (
        spread, spread, spread, P("seq", None, "batch"), P(None, "seq"), P(None, "seq"), P("seq")
    )
    return jax.shard_map(
        per_device, mesh=mesh, in_specs=in_specs, out_specs=out_specs, check_vma=False
    )
```
